32 devices in a mesh: angle: 4 (over y, core), tile: 8 (over z, x).
Axes of the slice: x: 2, y: 2, z: 4, core: 2. Of those that a mesh axis runs over, the one named last changes fastest.
Arguments:
- psi: float32 [2, 4, 160, 1024], P(None, 'angle', None, 'tile'), may hold values from -6 to 6
- target: float32 [2, 4, 160, 1024], P(None, 'angle', None, 'tile'), may hold values from -6 to 6
- probe: float32 [2, 128, 128], replicated, may hold values from -4.2 to 4.2
- data: float32 [4, 8, 16, 128, 128], P('angle', 'tile'), may hold values from 0.1 to 10
- pos_z: int32 [4, 8, 16], P('angle', 'tile'), may hold values from 0 to 32
- pos_x: int32 [4, 8, 16], P('angle', 'tile'), may hold values from 0 to 127
- counts: int32 [4, 8], P('angle', 'tile'), may hold values from 1 to 16, as said below
- shears: float32 [4], P('angle'), may hold values from -1 to 1
Outputs:
- psi_new: float32 [2, 4, 160, 1024], P(None, 'angle', None, 'tile')
- probe_new: float32 [2, 128, 128], replicated
- tomo_grad: bfloat16 [2, 160, 128, 1024], P(None, 'tile', 'angle')
The draws below stay inside these ranges and needn't reach their ends.
Inputs may be any that keep to these rules, and one draw needn't show every extreme that they name: counts[a, t] positions of angle a lie in tile t, in slots 0 to counts[a, t] - 1; later slots are unused. Some tile of some angle has exactly 16 in every draw.
All inputs are finite; a program needn't handle non-finite values.
Results may differ from the reference program's by a relative error of at most 0.001.
Values sent between devices are 32-bit elements; how exact they have to be, the bound alone decides.
No kernel may reach another device: no remote copies, remote signals or barrier semaphores. Data moves between devices by JAX's collectives and lax.ppermute only.
A program may use at most 192 MiB of HBM per device.

```python
import math
import jax
import jax.numpy as jnp
from jax import lax

PS = 128
TW = 128
CAP = 16
ZWIN = 160
ITERS = 2
ANG = 4
TILES = 8
H = 1024
Y = 128
N_TILE = 8


def draw_counts(key, part):
    first_key, second_key, third_key = jax.random.split(jax.random.fold_in(key, 7103), 3)
    first = jax.random.randint(first_key, (ANG, TILES), 0, CAP)
    second = jax.random.randint(second_key, (ANG, TILES), 0, CAP)
    values = jnp.minimum(first, second) + 1
    chosen = jax.random.randint(third_key, (), 0, ANG * TILES)
    flat_index = jnp.arange(ANG * TILES, dtype=jnp.int32).reshape(ANG, TILES)
    return jnp.where(flat_index == chosen, CAP, values).astype(jnp.int32)


def plant(drawn, stream_key, smallest, high):
    extent = drawn.shape
    place = [jax.random.randint(jax.random.fold_in(stream_key, axis), (), 0, extent[axis]) for axis in range(len(extent))]
    drawn = drawn.at[tuple(place)].set(smallest)
    longest = extent.index(max(extent))
    place[longest] = (place[longest] + 1) % extent[longest]
    return drawn.at[tuple(place)].set(high)


def block_levels(key, extent, cuts, least, largest):
    def one(axis_at, blocks):
        steps = jax.random.uniform(jax.random.fold_in(jax.random.fold_in(key, 6), axis_at), (blocks,), jnp.float32, least / len(cuts), largest / len(cuts))
        return jnp.repeat(jnp.exp(steps), extent[axis_at] // blocks).reshape((-1,) + (1,) * (len(extent) - axis_at - 1))

    level = one(*cuts[0])
    for cut in cuts[1:]:
        level = level * one(*cut)
    return level


def normal_values(own_key, shape, deviation, limit, shards=(), kind=jnp.bfloat16):
    result = deviation * jax.random.normal(own_key, shape, jnp.float32)
    if shards:
        result = result * block_levels(own_key, shape, shards, -0.22, 0.18)
    return jnp.clip(result, -limit, limit).astype(kind)


def setup_inputs(seed: int = 0) -> dict:
    seeds = jax.random.split(jax.random.key(seed), 9)
    psi = normal_values(seeds[0], (2, ANG, ZWIN, H), 1.0, 6.0, ((1, 4), (3, 8)), jnp.float32)
    target = normal_values(seeds[1], (2, ANG, ZWIN, H), 1.0, 6.0, ((1, 4), (3, 8)), jnp.float32)
    probe = normal_values(seeds[2], (2, PS, PS), 0.7, 4.2, (), jnp.float32)
    data = jnp.clip(jnp.exp(math.log(10.0) - 4.6051702 * jax.random.uniform(seeds[3], (ANG, TILES, CAP, PS, PS), jnp.float32) ** block_levels(seeds[3], (ANG, TILES, CAP, PS, PS), ((0, 4), (1, 8)), -0.2, 0.2)), 0.1, 10.0)
    pos_z = plant(jax.random.randint(seeds[4], (ANG, TILES, CAP), 0, ZWIN - PS + 1), jax.random.fold_in(seeds[4], 1), 0, ZWIN - PS).astype(jnp.int32)
    pos_x = plant(jax.random.randint(seeds[5], (ANG, TILES, CAP), 0, TW), jax.random.fold_in(seeds[5], 1), 0, TW - 1).astype(jnp.int32)
    counts = draw_counts(jax.random.fold_in(seeds[8], 71), 0)
    shears = jnp.clip(jax.random.uniform(seeds[7], (ANG,), jnp.float32, -1.0, 1.0) * block_levels(seeds[7], (ANG,), ((0, 4),), -0.4, 0.0), -1.0, 1.0)
    return {"psi": psi, "target": target, "probe": probe, "data": data, "pos_z": pos_z, "pos_x": pos_x, "counts": counts, "shears": shears}


ALPHA = 0.004
RHO = 5.0
PROBE_STEP = 0.02


def reference(psi, target, probe, data, pos_z, pos_x, counts, shears):
    half = PS // 2
    slot_mask = (jnp.arange(CAP, dtype=jnp.int32)[None, None, :] < counts[:, :, None]).astype(jnp.float32)
    tile_start = (jnp.arange(N_TILE, dtype=jnp.int32) * TW)[None, :, None]
    starts_x = (pos_x + tile_start).reshape(ANG, -1).astype(jnp.int32)
    starts_z = pos_z.reshape(ANG, -1).astype(jnp.int32)
    total_count = jnp.sum(counts).astype(jnp.float32)
    data_flat = data.reshape(ANG, -1, PS, PS)
    mask_flat = slot_mask.reshape(ANG, -1)
    field = psi
    probe_now = probe
    for step in range(ITERS):
        padded = jnp.pad(field, ((0, 0), (0, 0), (0, 0), (half, half)))
        probe_cplx = lax.complex(probe_now[0], probe_now[1])

        def one_angle(items):
            plane, data_one, zs_one, xs_one, mask_one = items
            plane_cplx = lax.complex(plane[0], plane[1])

            def cut_window(start_z, start_x):
                return lax.dynamic_slice(plane_cplx, (start_z, start_x), (PS, PS))

            patches = jax.vmap(cut_window)(zs_one, xs_one)
            far = jnp.fft.fft2(probe_cplx * patches, norm="ortho")
            misfit = (jnp.real(far) ** 2 + jnp.imag(far) ** 2 - data_one) * mask_one[:, None, None]
            back = jnp.fft.ifft2(misfit * far, norm="ortho")
            grads = jnp.conj(probe_cplx) * back
            probe_part = jnp.sum(jnp.conj(patches) * back, 0)

            def add_window(total, item):
                piece, start_z, start_x = item
                current = lax.dynamic_slice(total, (start_z, start_x), (PS, PS))
                return lax.dynamic_update_slice(total, current + piece, (start_z, start_x)), None

            total, unused = lax.scan(add_window, jnp.zeros_like(plane_cplx), (grads, zs_one, xs_one))
            return (jnp.stack([jnp.real(total), jnp.imag(total)]),
                    jnp.stack([jnp.real(probe_part), jnp.imag(probe_part)]))

        grads, probe_parts = lax.map(one_angle, (jnp.moveaxis(padded, 1, 0), data_flat, starts_z, starts_x, mask_flat))
        grad_field = jnp.moveaxis(grads, 0, 1)[:, :, :, half:half + H]
        new_field = field - ALPHA * (grad_field + RHO * (field - target))
        probe_now = probe_now - PROBE_STEP * jnp.sum(probe_parts, 0) / total_count
        field = new_field
    gap = target - field
    spectrum = jnp.fft.fft(lax.complex(gap[0], gap[1]), axis=-1)
    freq = jnp.arange(H, dtype=jnp.int32)
    signed = jnp.where(freq < H // 2, freq, freq - H)
    offsets = jnp.arange(Y, dtype=jnp.int32) - Y // 2
    product = (offsets[:, None] * signed[None, :]).astype(jnp.float32)
    theta = (product[None, :, :] * shears[:, None, None]) * (2.0 * math.pi / H)
    table = lax.complex(jnp.cos(theta), jnp.sin(theta))

    def one_slice(spec_row):
        summed = jnp.sum(table * spec_row[:, None, :], 0)
        values = jnp.fft.ifft(summed, axis=-1) / ANG
        return jnp.stack([jnp.real(values), jnp.imag(values)]).astype(jnp.bfloat16)

    tomo = lax.map(one_slice, jnp.moveaxis(spectrum, 1, 0))
    return field, probe_now, jnp.moveaxis(tomo, 0, 1)
```

```python
import functools
import math

import jax
import jax.numpy as jnp
import ml_dtypes
import numpy as np
from jax import lax
from jax.experimental import pallas as pl
from jax.experimental.pallas import tpu as pltpu
from jax.sharding import PartitionSpec as P

ITERS = 2
ALPHA = 0.004
RHO = 5.0
PROBE_STEP = 0.02
GROUP = 4
VMEM_LIMIT = 40 * 1024 * 1024
BF16 = jnp.bfloat16
F32 = jnp.float32


def split_table(matrix, axis):
    high = matrix.astype(ml_dtypes.bfloat16)
    low = (matrix - high.astype(np.float64)).astype(ml_dtypes.bfloat16)
    return np.concatenate([high, high, low], axis)


def dft_parts(length, orient, scale):
    counter = np.arange(length)
    angle = 2.0 * math.pi / length * (np.outer(counter, counter) % length)
    return np.cos(angle) * scale, orient * np.sin(angle) * scale


def right_table(length, orient, scale):
    real, imag = dft_parts(length, orient, scale)
    return split_table(np.block([[real, imag], [-imag, real]]), 0)


def left_table(length, orient, scale):
    real, imag = dft_parts(length, orient, scale)
    return split_table(np.block([[real, -imag], [imag, real]]), 1)


def twiddles(tiles, inner, orient, scale):
    angle = 2.0 * math.pi / (tiles * inner) * np.outer(np.arange(tiles), np.arange(inner))
    return np.stack([np.cos(angle) * scale, orient * np.sin(angle) * scale]).astype(np.float32)


def halves(value):
    high = value.astype(BF16)
    low = (value - high.astype(F32)).astype(BF16)
    return high, low


def dot(left, right):
    return jnp.dot(left, right, preferred_element_type=F32)


def butterfly(parts, orient):
    count = len(parts)
    if count == 1:
        return parts
    even = butterfly(parts[0::2], orient)
    odd = butterfly(parts[1::2], orient)
    low, high = [], []
    for index in range(count // 2):
        angle = orient * 2.0 * math.pi * index / count
        real, imag = odd[index]
        if index == 0:
            turned = (real, imag)
        elif 4 * index == count:
            turned = (-imag, real) if orient > 0 else (imag, -real)
        else:
            cosine, sine = math.cos(angle), math.sin(angle)
            turned = (real * cosine - imag * sine, real * sine + imag * cosine)
        base_real, base_imag = even[index]
        low.append((base_real + turned[0], base_imag + turned[1]))
        high.append((base_real - turned[0], base_imag - turned[1]))
    return low + high


def lane_mask(shape, half):
    return lax.broadcasted_iota(jnp.int32, shape, len(shape) - 1) < half


def slot_loop(pos_z, pos_x, count, probe_real, probe_imag, data, tables, own, halo, work):
    right_fwd, left_fwd, left_inv, right_inv = tables
    grad_own, grad_halo, grad_probe, patches, high_rows, low_rows = work
    side = data.shape[-1]
    half = side // 2
    lanes = lax.broadcasted_iota(jnp.int32, (side, side), 1)
    grad_own[...] = jnp.zeros_like(grad_own)
    grad_halo[...] = jnp.zeros_like(grad_halo)
    grad_probe[...] = jnp.zeros_like(grad_probe)

    def place(slot):
        start = pos_x[0, 0, slot] - half
        back = jnp.where(start > 0, side - start, -start)
        forth = jnp.where(start < 0, side + start, start)
        inside = (lanes >= start) & (lanes < side + start)
        return pos_z[0, 0, slot], back, forth, inside

    def group(index, carry):
        first = index * GROUP
        for member in range(GROUP):
            row, back, _, inside = place(first + member)
            cut = []
            for part in range(2):
                mixed = jnp.where(
                    inside, own[part, pl.ds(row, side), :], halo[part, pl.ds(row, side), :]
                )
                cut.append(pltpu.roll(mixed, back, 1))
                patches[member, part] = cut[part]
            exit_wave = jnp.concatenate(
                [
                    probe_real[...] * cut[0] - probe_imag[...] * cut[1],
                    probe_real[...] * cut[1] + probe_imag[...] * cut[0],
                ],
                1,
            )
            high, low = halves(exit_wave)
            high_rows[pl.ds(member * side, side), :] = high
            low_rows[pl.ds(member * side, side), :] = low
        high, low = high_rows[...], low_rows[...]
        rows = dot(jnp.concatenate([high, low, high], 1), right_fwd[...])
        for pair in range(GROUP // 2):
            two = [rows[(2 * pair + k) * side : (2 * pair + k + 1) * side] for k in range(2)]
            stacked = jnp.concatenate(
                [
                    jnp.concatenate([block[:, :side] for block in two], 1),
                    jnp.concatenate([block[:, side:] for block in two], 1),
                ],
                0,
            )
            high, low = halves(stacked)
            far = dot(left_fwd[...], jnp.concatenate([high, low, high], 0))
            weights = []
            for k in range(2):
                slot = first + 2 * pair + k
                live = jnp.where(slot < count, 1.0, 0.0).astype(F32)
                far_real = far[:side, k * side : (k + 1) * side]
                far_imag = far[side:, k * side : (k + 1) * side]
                weights.append((far_real * far_real + far_imag * far_imag - data[0, 0, slot]) * live)
            weight = jnp.concatenate(weights, 1)
            high, low = halves(jnp.concatenate([far[:side] * weight, far[side:] * weight], 0))
            back_cols = dot(left_inv[...], jnp.concatenate([high, low, high], 0))
            for k in range(2):
                block = back_cols[:, k * side : (k + 1) * side]
                high, low = halves(jnp.concatenate([block[:side], block[side:]], 1))
                high_rows[pl.ds((2 * pair + k) * side, side), :] = high
                low_rows[pl.ds((2 * pair + k) * side, side), :] = low
        high, low = high_rows[...], low_rows[...]
        chi = dot(jnp.concatenate([high, low, high], 1), right_inv[...])
        sum_real, sum_imag = grad_probe[0], grad_probe[1]
        for member in range(GROUP):
            row, _, forth, inside = place(first + member)
            chi_real = chi[member * side : (member + 1) * side, :side]
            chi_imag = chi[member * side : (member + 1) * side, side:]
            cut_real, cut_imag = patches[member, 0], patches[member, 1]
            sum_real = sum_real + (cut_real * chi_real + cut_imag * chi_imag)
            sum_imag = sum_imag + (cut_real * chi_imag - cut_imag * chi_real)
            grads = (
                probe_real[...] * chi_real + probe_imag[...] * chi_imag,
                probe_real[...] * chi_imag - probe_imag[...] * chi_real,
            )
            for part in range(2):
                moved = pltpu.roll(grads[part], forth, 1)
                where = pl.ds(row, side)
                grad_own[part, where, :] += jnp.where(inside, moved, 0.0)
                grad_halo[part, where, :] += jnp.where(inside, 0.0, moved)
        grad_probe[0], grad_probe[1] = sum_real, sum_imag
        return carry

    lax.fori_loop(0, (count + GROUP - 1) // GROUP, group, 0)


def first_kernel(
    pos_z, pos_x, counts, shears, psi, target, left, right, probe, data, *rest
):
    tables = rest[:4]
    to_right, to_left, base_out, rim_out, sums_out = rest[4:9]
    halo, work = rest[9], rest[10:]
    grad_own, grad_halo, grad_probe = work[:3]
    side = data.shape[-1]
    mask = lane_mask(psi.shape[2:], side // 2)
    for part in range(2):
        halo[part] = jnp.where(mask, right[part, 0], left[part, 0])
    count = counts[0, 0]
    slot_loop(
        pos_z, pos_x, count, probe.at[0], probe.at[1], data, tables, psi.at[:, 0], halo, work
    )
    for part in range(2):
        field = psi[part, 0]
        base = field - ALPHA * (grad_own[part] + RHO * (field - target[part, 0]))
        rim = -ALPHA * grad_halo[part]
        base_out[part] = base
        rim_out[part] = rim
        to_right[part] = jnp.where(mask, rim, base)
        to_left[part] = jnp.where(mask, base, rim)
    devices, rows = sums_out.shape[0], sums_out.shape[1] - 8
    extra = jnp.where(
        lax.broadcasted_iota(jnp.int32, (8, side), 0) == 0,
        jnp.full((8, side), count.astype(F32)),
        jnp.full((8, side), shears[0]),
    )
    per_part = side // rows
    for device in range(devices):
        part, place = device // per_part, device % per_part
        sums_out[device, 0:rows] = grad_probe[part, place * rows : (place + 1) * rows]
        sums_out[device, rows : rows + 8] = extra


def chunk_kernel(received, probe, chunk_out, total_out):
    devices, rows = chunk_out.shape[0], chunk_out.shape[1]
    total = received[0]
    for device in range(1, devices):
        total = total + received[device]
    number = total[rows : rows + 1]
    me = lax.axis_index("angle") * lax.axis_size("tile") + lax.axis_index("tile")
    mine = probe[pl.ds(me, 1)][0] - PROBE_STEP * total[:rows] / number
    for device in range(devices):
        chunk_out[device] = mine
    total_out[...] = jnp.broadcast_to(number, total_out.shape)


def second_kernel(
    pos_z, pos_x, counts, base, rim, left, right, target, probe, data, *rest
):
    tables = rest[:4]
    slabs_out, base_out, rim_out = rest[4:7]
    own, halo, hold, work = rest[7], rest[8], rest[9], rest[10:]
    grad_own, grad_halo, grad_probe = work[:3]
    side = data.shape[-1]
    mask = lane_mask(base.shape[1:], side // 2)
    tile, tiles = lax.axis_index("tile"), lax.axis_size("tile")
    from_right = jnp.where(tile < tiles - 1, 1.0, 0.0).astype(F32)
    from_left = jnp.where(tile > 0, 1.0, 0.0).astype(F32)
    for part in range(2):
        own[part] = base[part] + jnp.where(mask, left[part], right[part])
        halo[part] = jnp.where(
            mask,
            (right[part] + rim[part]) * from_right,
            (left[part] + rim[part]) * from_left,
        )
    slot_loop(
        pos_z, pos_x, counts[0, 0], probe.at[0], probe.at[1], data, tables, own, halo, work
    )
    slabs, depth = slabs_out.shape[0], base.shape[1] // slabs_out.shape[0]
    chunk = slabs_out.shape[1] - 4 * depth
    for part in range(2):
        field = own[part]
        aim = target[part, 0]
        updated = field - ALPHA * (grad_own[part] + RHO * (field - aim))
        edge = -ALPHA * grad_halo[part]
        base_out[part] = updated
        rim_out[part] = edge
        hold[part] = aim - updated
    per_part = side // chunk
    for slab in range(slabs):
        rows = pl.ds(slab * depth, depth)
        for part in range(2):
            slabs_out[slab, part * depth : (part + 1) * depth] = hold[part, rows]
            slabs_out[slab, (2 + part) * depth : (3 + part) * depth] = rim_out[part, rows]
        part, place = slab // per_part, slab % per_part
        slabs_out[slab, 4 * depth : 4 * depth + chunk] = grad_probe[
            part, place * chunk : (place + 1) * chunk
        ]


def forward_kernel(slabs, turn, table, spectrum_out, rows_scratch):
    tiles, height, width = slabs.shape
    depth = rows_scratch.shape[0] // tiles
    chunk = height - 4 * depth
    mask = lane_mask((depth, width), width // 2)
    blocks = []
    for tile in range(tiles):
        block = []
        for part in range(2):
            rows = slice((2 + part) * depth, (3 + part) * depth)
            zero = jnp.zeros((depth, width), F32)
            before = slabs[tile - 1, rows] if tile > 0 else zero
            after = slabs[tile + 1, rows] if tile < tiles - 1 else zero
            block.append(
                slabs[tile, part * depth : (part + 1) * depth] - jnp.where(mask, before, after)
            )
        blocks.append(tuple(block))
    for index, (real, imag) in enumerate(butterfly(blocks, -1)):
        cosine, sine = turn[0, index : index + 1], turn[1, index : index + 1]
        rows = slice(index * depth, (index + 1) * depth)
        rows_scratch[rows, :width] = real * cosine - imag * sine
        rows_scratch[rows, width:] = real * sine + imag * cosine
    high, low = halves(rows_scratch[...])
    spectrum = dot(jnp.concatenate([high, low, high], 1), table[...])
    count = rows_scratch.shape[0]
    spectrum_out[0:count] = spectrum[:, :width]
    spectrum_out[count : 2 * count] = spectrum[:, width:]
    total = slabs[0, 4 * depth : 4 * depth + chunk]
    for tile in range(1, tiles):
        total = total + slabs[tile, 4 * depth : 4 * depth + chunk]
    spectrum_out[2 * count : 2 * count + chunk] = total


def phase_kernel(tiles, received, table_out):
    angles, _, _, beam, width = table_out.shape
    rows = received.shape[1] - 8
    total = tiles * width
    first = lax.axis_index("angle") * beam - (beam * lax.axis_size("angle")) // 2
    offsets = (lax.broadcasted_iota(jnp.int32, (beam, width), 0) + first).astype(F32)
    column = lax.broadcasted_iota(jnp.int32, (beam, width), 1)
    for angle in range(angles):
        shear = received[angle * tiles, rows + 1 : rows + 2]
        for block in range(tiles):
            frequency = block + tiles * column
            signed = jnp.where(frequency < total // 2, frequency, frequency - total).astype(F32)
            turns = (offsets * signed * shear) * (1.0 / total)
            turns = turns - jnp.floor(turns + 0.5)
            x = turns * math.pi
            square = x * x
            sine = x * (
                1.0 + square * (-1 / 6 + square * (1 / 120 + square * (-1 / 5040 + square * (
                    1 / 362880 + square * (-1 / 39916800 + square * (1.0 / 6227020800.0))))))
            )
            cosine = 1.0 + square * (-1 / 2 + square * (1 / 24 + square * (-1 / 720 + square * (
                1 / 40320 + square * (-1 / 3628800 + square * (1.0 / 479001600.0))))))
            table_out[angle, 0, block] = 1.0 - 2.0 * sine * sine
            table_out[angle, 1, block] = 2.0 * sine * cosine


def inverse_kernel(depth, spectra, phases, turn, table, image_out, high_rows, low_rows):
    angles, _, tiles, beam, width = phases.shape
    row = pl.program_id(0)
    count = tiles * depth
    for block in range(tiles):
        real = jnp.zeros((beam, width), F32)
        imag = jnp.zeros((beam, width), F32)
        for angle in range(angles):
            spec_real = spectra[angle, pl.ds(block * depth + row, 1), :]
            spec_imag = spectra[angle, pl.ds(count + block * depth + row, 1), :]
            cosine, sine = phases[angle, 0, block], phases[angle, 1, block]
            real = real + (cosine * spec_real - sine * spec_imag)
            imag = imag + (cosine * spec_imag + sine * spec_real)
        rows = slice(block * beam, (block + 1) * beam)
        for part, value in enumerate((real, imag)):
            high, low = halves(value)
            high_rows[rows, part * width : (part + 1) * width] = high
            low_rows[rows, part * width : (part + 1) * width] = low
    high, low = high_rows[...], low_rows[...]
    image = dot(jnp.concatenate([high, low, high], 1), table[...])
    blocks = []
    for block in range(tiles):
        real = image[block * beam : (block + 1) * beam, :width]
        imag = image[block * beam : (block + 1) * beam, width:]
        cosine, sine = turn[0, block : block + 1], turn[1, block : block + 1]
        blocks.append((real * cosine - imag * sine, real * sine + imag * cosine))
    for index, (real, imag) in enumerate(butterfly(blocks, 1)):
        columns = slice(index * width, (index + 1) * width)
        image_out[0, 0, :, columns] = real.astype(BF16)
        image_out[1, 0, :, columns] = imag.astype(BF16)


def last_kernel(probe_rows, spectra, probe, number, base, left, right, chunk_out, psi_out):
    angles, tiles, rows = spectra.shape[0], chunk_out.shape[0], chunk_out.shape[1]
    total = spectra[0, probe_rows : probe_rows + rows]
    for angle in range(1, angles):
        total = total + spectra[angle, probe_rows : probe_rows + rows]
    tile = lax.axis_index("tile")
    mine = probe[pl.ds(tile, 1)][0] - PROBE_STEP * total / number[0:1]
    for place in range(tiles):
        chunk_out[place] = mine
    mask = lane_mask(base.shape[1:], base.shape[-1] // 2)
    for part in range(2):
        psi_out[part, 0] = base[part] + jnp.where(mask, left[part], right[part])


VMEM = pl.BlockSpec(memory_space=pltpu.VMEM)
SMEM = pl.BlockSpec(memory_space=pltpu.SMEM)


def call(body, name, out_shape, in_specs, scratch=(), flops=0, size=0, **more):
    return pl.pallas_call(
        body,
        name=name,
        out_shape=out_shape,
        in_specs=in_specs,
        scratch_shapes=list(scratch),
        compiler_params=pltpu.CompilerParams(vmem_limit_bytes=VMEM_LIMIT),
        cost_estimate=pl.CostEstimate(flops=flops, bytes_accessed=size, transcendentals=0),
        **more,
    )


def shape(*dims, dtype=F32):
    return jax.ShapeDtypeStruct(dims, dtype)


def shards(psi, target, probe, data, pos_z, pos_x, counts, shears):
    rows_total, width = psi.shape[2], psi.shape[3]
    side = probe.shape[1]
    angles, tiles = lax.axis_size("angle"), lax.axis_size("tile")
    devices = angles * tiles
    depth = rows_total // tiles
    beam = 32
    both = ("angle", "tile")
    forward = [(i, i + 1) for i in range(tiles - 1)]
    backward = [(i + 1, i) for i in range(tiles - 1)]
    norm = 1.0 / math.sqrt(side)
    tables = [
        jnp.asarray(right_table(side, -1.0, norm)),
        jnp.asarray(left_table(side, -1.0, norm)),
        jnp.asarray(left_table(side, 1.0, norm)),
        jnp.asarray(right_table(side, 1.0, norm)),
    ]
    block = (2, rows_total, width)
    work = [
        pltpu.VMEM(block, F32),
        pltpu.VMEM(block, F32),
        pltpu.VMEM((2, side, side), F32),
        pltpu.VMEM((GROUP, 2, side, side), F32),
        pltpu.VMEM((GROUP * side, 2 * side), BF16),
        pltpu.VMEM((GROUP * side, 2 * side), BF16),
    ]
    slots = data.shape[2]
    flops = slots * 4 * 2 * side * 6 * side * 2 * side
    left = lax.ppermute(psi, "tile", forward)
    right = lax.ppermute(psi, "tile", backward)
    chunk = 2 * side // devices
    to_right, to_left, base, rim, sums = call(
        first_kernel,
        "ptycho_first",
        [shape(*block)] * 4 + [shape(devices, chunk + 8, side)],
        [SMEM] * 4 + [VMEM] * 10,
        [pltpu.VMEM(block, F32)] + work,
        flops,
    )(pos_z, pos_x, counts, shears, psi, target, left, right, probe, data, *tables)
    left = lax.ppermute(to_right, "tile", forward)
    right = lax.ppermute(to_left, "tile", backward)
    received = lax.all_to_all(sums, both, 0, 0, tiled=True)
    chunks, number = call(
        chunk_kernel,
        "probe_chunk",
        [shape(devices, chunk, side), shape(8, side)],
        [VMEM] * 2,
    )(received, probe.reshape(devices, chunk, side))
    probe_one = lax.all_to_all(chunks, both, 0, 0, tiled=True).reshape(2, side, side)
    phases = call(
        functools.partial(phase_kernel, tiles),
        "phase_table",
        shape(angles, 2, tiles, beam, width),
        [VMEM],
        (),
        angles * tiles * beam * width * 40,
    )(received)
    piece = 2 * side // tiles
    slabs, base, rim = call(
        second_kernel,
        "ptycho_second",
        [shape(tiles, 4 * depth + piece, width), shape(*block), shape(*block)],
        [SMEM] * 3 + [VMEM] * 11,
        [pltpu.VMEM(block, F32)] * 3 + work,
        flops,
    )(pos_z, pos_x, counts, base, rim, left, right, target, probe_one, data, *tables)
    slabs = lax.all_to_all(slabs, "tile", 0, 0, tiled=True)
    left = lax.ppermute(rim, "tile", forward)
    right = lax.ppermute(rim, "tile", backward)
    count = tiles * depth
    spectrum = call(
        forward_kernel,
        "slab_spectrum",
        shape(2 * count + piece, width),
        [VMEM] * 3,
        [pltpu.VMEM((count, 2 * width), F32)],
    )(slabs, jnp.asarray(twiddles(tiles, width, -1.0, 1.0)), jnp.asarray(right_table(width, -1.0, 1.0)))
    spectra = lax.all_gather(spectrum, "angle", axis=0, tiled=False)
    chunks, psi_new = call(
        functools.partial(last_kernel, 2 * count),
        "probe_last",
        [shape(tiles, piece, side), shape(2, 1, rows_total, width)],
        [VMEM] * 6,
    )(spectra, probe_one.reshape(tiles, piece, side), number, base, left, right)
    probe_new = lax.all_to_all(chunks, "tile", 0, 0, tiled=True).reshape(2, side, side)
    scale = 1.0 / (angles * tiles * width)
    tomo = call(
        functools.partial(inverse_kernel, depth),
        "slab_image",
        shape(2, depth, beam, tiles * width, dtype=BF16),
        [VMEM] * 4,
        [pltpu.VMEM((tiles * beam, 2 * width), BF16)] * 2,
        depth * tiles * beam * 2 * 6 * width * 2 * width,
        grid=(depth,),
        out_specs=pl.BlockSpec((2, 1, beam, tiles * width), lambda row: (0, row, 0, 0)),
    )(
        spectra,
        phases,
        jnp.asarray(twiddles(tiles, width, 1.0, scale)),
        jnp.asarray(right_table(width, 1.0, 1.0)),
    )
    return psi_new, probe_new, tomo


def solution(mesh):
    in_specs = (
        P(None, "angle", None, "tile"),
        P(None, "angle", None, "tile"),
        P(),
        P("angle", "tile", None, None, None),
        P("angle", "tile", None),
        P("angle", "tile", None),
        P("angle", "tile"),
        P("angle"),
    )
    out_specs = (P(None, "angle", None, "tile"), P(), P(None, "tile", "angle", None))
    return jax.shard_map(shards, mesh=mesh, in_specs=in_specs, out_specs=out_specs, check_vma=False)
```

```python
import functools
import math

import jax
import jax.numpy as jnp
import ml_dtypes
import numpy as np
from jax import lax
from jax.experimental import pallas as pl
from jax.experimental.pallas import tpu as pltpu
from jax.sharding import PartitionSpec as P

ITERS = 2
ALPHA = 0.004
RHO = 5.0
PROBE_STEP = 0.02
GROUP = 4
VMEM_LIMIT = 40 * 1024 * 1024
BF16 = jnp.bfloat16
F32 = jnp.float32


def split_table(matrix, axis):
    high = matrix.astype(ml_dtypes.bfloat16)
    low = (matrix - high.astype(np.float64)).astype(ml_dtypes.bfloat16)
    return np.concatenate([high, high, low], axis)


def dft_parts(length, orient, scale):
    counter = np.arange(length)
    angle = 2.0 * math.pi / length * (np.outer(counter, counter) % length)
    return np.cos(angle) * scale, orient * np.sin(angle) * scale


def right_table(length, orient, scale):
    real, imag = dft_parts(length, orient, scale)
    return split_table(np.block([[real, imag], [-imag, real]]), 0)


def left_table(length, orient, scale):
    real, imag = dft_parts(length, orient, scale)
    matrix = np.block([[real, -imag], [imag, real]])
    high = matrix.astype(ml_dtypes.bfloat16)
    return np.concatenate([high, (matrix - high.astype(np.float64)).astype(ml_dtypes.bfloat16)], 0)


def twiddles(tiles, inner, orient, scale):
    angle = 2.0 * math.pi / (tiles * inner) * np.outer(np.arange(tiles), np.arange(inner))
    return np.stack([np.cos(angle) * scale, orient * np.sin(angle) * scale]).astype(np.float32)


def halves(value):
    high = value.astype(BF16)
    low = (value - high.astype(F32)).astype(BF16)
    return high, low


def dot(left, right):
    return jnp.dot(left, right, preferred_element_type=F32)


def tall(table, high, low):
    size = high.shape[0]
    both = dot(table[...], high)
    return both[:size] + both[size:] + dot(table[0:size], low)


def butterfly(parts, orient):
    count = len(parts)
    if count == 1:
        return parts
    even = butterfly(parts[0::2], orient)
    odd = butterfly(parts[1::2], orient)
    low, high = [], []
    for index in range(count // 2):
        angle = orient * 2.0 * math.pi * index / count
        real, imag = odd[index]
        if index == 0:
            turned = (real, imag)
        elif 4 * index == count:
            turned = (-imag, real) if orient > 0 else (imag, -real)
        else:
            cosine, sine = math.cos(angle), math.sin(angle)
            turned = (real * cosine - imag * sine, real * sine + imag * cosine)
        base_real, base_imag = even[index]
        low.append((base_real + turned[0], base_imag + turned[1]))
        high.append((base_real - turned[0], base_imag - turned[1]))
    return low + high


def lane_mask(shape, half):
    return lax.broadcasted_iota(jnp.int32, shape, len(shape) - 1) < half


def side_by_side(stages, count, group):
    groups = count // group
    held = [None] * groups
    for turn in range(groups + len(stages) - 1):
        for number in reversed(range(len(stages))):
            at = turn - number
            if 0 <= at < groups:
                held[at] = stages[number](at * group, held[at])


def slot_loop(pos_z, pos_x, count, probe_real, probe_imag, data, tables, own, halo, work):
    right_fwd, left_fwd, left_inv, right_inv = tables
    grad_own, grad_halo, grad_probe, patches = work
    side = data.shape[-1]
    half = side // 2
    slots = data.shape[2]
    group = math.gcd(slots, GROUP)
    wide = math.gcd(group, 2)
    lanes = lax.broadcasted_iota(jnp.int32, (side, side), 1)
    grad_own[...] = jnp.zeros_like(grad_own)
    grad_halo[...] = jnp.zeros_like(grad_halo)
    grad_probe[...] = jnp.zeros_like(grad_probe)

    def place(slot):
        start = pos_x[0, 0, slot] - half
        back = jnp.where(start > 0, side - start, -start)
        forth = jnp.where(start < 0, side + start, start)
        inside = (lanes >= start) & (lanes < side + start)
        return pl.ds(pos_z[0, 0, slot], side), back, forth, inside

    def cut_out(first, _):
        waves = []
        for slot in range(first, first + group):
            where, back, _, inside = place(slot)
            cut = []
            for part in range(2):
                mixed = jnp.where(inside, own[part, where, :], halo[part, where, :])
                cut.append(pltpu.roll(mixed, back, 1))
                patches[slot, part] = cut[part]
            waves.append(
                jnp.concatenate(
                    [
                        probe_real[...] * cut[0] - probe_imag[...] * cut[1],
                        probe_real[...] * cut[1] + probe_imag[...] * cut[0],
                    ],
                    1,
                )
            )
        return halves(jnp.concatenate(waves, 0))

    def rows_forward(first, split):
        high, low = split
        rows = dot(jnp.concatenate([high, low, high], 1), right_fwd[...])
        stacks = []
        for at in range(0, group, wide):
            some = [rows[(at + k) * side : (at + k + 1) * side] for k in range(wide)]
            stacked = jnp.concatenate(
                [
                    jnp.concatenate([block[:, :side] for block in some], 1),
                    jnp.concatenate([block[:, side:] for block in some], 1),
                ],
                0,
            )
            stacks.append(halves(stacked))
        return stacks

    def columns_forward(first, stacks):
        results = []
        for index, (high, low) in enumerate(stacks):
            far = tall(left_fwd, high, low)
            weights = []
            for k in range(wide):
                slot = first + index * wide + k
                live = jnp.where(slot < count, 1.0, 0.0).astype(F32)
                far_real = far[:side, k * side : (k + 1) * side]
                far_imag = far[side:, k * side : (k + 1) * side]
                weights.append((far_real * far_real + far_imag * far_imag - data[0, 0, slot]) * live)
            weight = jnp.concatenate(weights, 1)
            results.append(halves(jnp.concatenate([far[:side] * weight, far[side:] * weight], 0)))
        return results

    def columns_inverse(first, stacks):
        blocks = []
        for high, low in stacks:
            back_cols = tall(left_inv, high, low)
            for k in range(wide):
                block = back_cols[:, k * side : (k + 1) * side]
                blocks.append(jnp.concatenate([block[:side], block[side:]], 1))
        return halves(jnp.concatenate(blocks, 0))

    def rows_inverse(first, split):
        high, low = split
        return dot(jnp.concatenate([high, low, high], 1), right_inv[...])

    def add_back(first, chi):
        sum_real, sum_imag = grad_probe[0], grad_probe[1]
        for member in range(group):
            slot = first + member
            where, _, forth, inside = place(slot)
            chi_real = chi[member * side : (member + 1) * side, :side]
            chi_imag = chi[member * side : (member + 1) * side, side:]
            cut_real, cut_imag = patches[slot, 0], patches[slot, 1]
            sum_real = sum_real + (cut_real * chi_real + cut_imag * chi_imag)
            sum_imag = sum_imag + (cut_real * chi_imag - cut_imag * chi_real)
            grads = (
                probe_real[...] * chi_real + probe_imag[...] * chi_imag,
                probe_real[...] * chi_imag - probe_imag[...] * chi_real,
            )
            for part in range(2):
                moved = pltpu.roll(grads[part], forth, 1)
                grad_own[part, where, :] += jnp.where(inside, moved, 0.0)
                grad_halo[part, where, :] += jnp.where(inside, 0.0, moved)
        grad_probe[0], grad_probe[1] = sum_real, sum_imag

    side_by_side(
        [cut_out, rows_forward, columns_forward, columns_inverse, rows_inverse, add_back], slots, group
    )


def stage_kernel(*refs):
    count = (len(refs) - 1) // 2
    copies = [
        pltpu.make_async_copy(refs[index], refs[count + index], refs[-1].at[index])
        for index in range(count)
    ]
    for copy in copies:
        copy.start()
    for copy in copies:
        copy.wait()


def sides(partner, other, part, even):
    first, second = partner[part], other[part]
    return jnp.where(even, second, first), jnp.where(even, first, second)


def is_even():
    return lax.axis_index("tile") % 2 == 0


def load_places(sources, targets, sems):
    copies = [
        pltpu.make_async_copy(source, target, sems.at[index])
        for index, (source, target) in enumerate(zip(sources, targets))
    ]
    for copy in copies:
        copy.start()
    return copies


def fold(kept, turned, mask):
    return jnp.where(mask, kept, pltpu.roll(turned, mask.shape[-1] // 2, 1))


def pack_kernel(psi, to_partner, to_other, held, sems):
    copies = [pltpu.make_async_copy(psi.at[part, 0], held.at[part], sems.at[part]) for part in range(2)]
    for copy in copies:
        copy.start()
    mask = lane_mask(to_partner.shape, to_partner.shape[-1] // 2)
    even = is_even()
    for copy in copies:
        copy.wait()
    to_left = fold(held[0], held[1], mask)
    to_right = fold(held[0], held[1], ~mask)
    to_partner[...] = jnp.where(even, to_right, to_left)
    to_other[...] = jnp.where(even, to_left, to_right)


def unfold(low_source, high_source, mask):
    real = jnp.where(mask, low_source, high_source)
    imag = pltpu.roll(jnp.where(mask, high_source, low_source), mask.shape[-1] // 2, 1)
    return real, imag


def packed_sides(partner, other, even):
    first, second = partner[...], other[...]
    return jnp.where(even, second, first), jnp.where(even, first, second)


def first_kernel(
    pos_z, pos_x, counts, shears, psi, target, partner, other, probe, data, *rest
):
    tables = rest[:4]
    to_partner, to_other, base_out, rim_out, keep_out, send_out = rest[4:10]
    held, sems, halo, work = rest[10:12], rest[12], rest[13], rest[14:]
    copies = load_places((pos_z, pos_x), held, sems)
    pos_z, pos_x = held
    grad_own, grad_halo, grad_probe = work[:3]
    side = data.shape[-1]
    mask = lane_mask(psi.shape[2:], side // 2)
    even = is_even()
    left, right = packed_sides(partner, other, even)
    halo[0], halo[1] = unfold(right, left, mask)
    for copy in copies:
        copy.wait()
    count = counts[0, 0]
    slot_loop(
        pos_z, pos_x, count, probe.at[0], probe.at[1], data, tables, psi.at[:, 0], halo, work
    )
    for part in range(2):
        field = psi[part, 0]
        base = field - ALPHA * (grad_own[part] + RHO * (field - target[part, 0]))
        rim = -ALPHA * grad_halo[part]
        base_out[part] = base
        rim_out[part] = rim
        to_right, to_left = jnp.where(mask, rim, base), jnp.where(mask, base, rim)
        to_partner[part] = jnp.where(even, to_right, to_left)
        to_other[part] = jnp.where(even, to_left, to_right)
    row = lax.broadcasted_iota(jnp.int32, (8, side), 0)
    lane = lax.broadcasted_iota(jnp.int32, (8, side), 1)
    angle, tile = lax.axis_index("angle"), lax.axis_index("tile")
    mine = (row == 1) & (lane == angle) & (tile == 0)
    extra = jnp.where(row == 0, count.astype(F32), jnp.where(mine, shears[0], 0.0))
    core = angle % 2
    for out, part in ((keep_out, core), (send_out, 1 - core)):
        out[0:side] = grad_probe[part]
        out[side : side + 8] = extra


def sum_kernel(*refs):
    terms = [ref[...] for ref in refs[:-1]]
    while len(terms) > 1:
        terms = [terms[at] + terms[at + 1] for at in range(0, len(terms), 2)]
    refs[-1][...] = terms[0]


def probe_kernel(probe, *refs):
    total, probe_out, extra_out = refs[-1], refs[-3], refs[-2]
    sum_kernel(*refs[:-3], total)
    side = probe.shape[-1]
    extra = total[side : side + 8]
    part = lax.axis_index("angle") % 2
    probe_out[...] = probe[part] - PROBE_STEP * total[0:side] / extra[0:1]
    extra_out[...] = extra


def second_kernel(
    pos_z, pos_x, counts, base, rim, partner, other, target, probe_mine, probe_theirs, data, *rest
):
    tables = rest[:4]
    slabs_out, base_out, to_partner, to_other, probe = rest[5:10]
    held, sems, own, halo, hold, edge, work = rest[10:12], *rest[12:17], rest[17:]
    copies = load_places((pos_z, pos_x), held, sems)
    pos_z, pos_x = held
    grad_own, grad_halo, grad_probe = work[:3]
    side = data.shape[-1]
    mask = lane_mask(base.shape[1:], side // 2)
    tile, tiles = lax.axis_index("tile"), lax.axis_size("tile")
    from_right = jnp.where(tile < tiles - 1, 1.0, 0.0).astype(F32)
    from_left = jnp.where(tile > 0, 1.0, 0.0).astype(F32)
    core = lax.axis_index("angle") % 2
    probe[core] = probe_mine[...]
    probe[1 - core] = probe_theirs[...]
    even = is_even()
    for part in range(2):
        left, right = sides(partner, other, part, even)
        own[part] = base[part] + jnp.where(mask, left, right)
        halo[part] = jnp.where(
            mask, (right + rim[part]) * from_right, (left + rim[part]) * from_left
        )
    for copy in copies:
        copy.wait()
    slot_loop(
        pos_z, pos_x, counts[0, 0], probe.at[0], probe.at[1], data, tables, own, halo, work
    )
    slabs, depth = slabs_out.shape[0], base.shape[1] // slabs_out.shape[0]
    chunk = slabs_out.shape[1] - 4 * depth
    for part in range(2):
        field = own[part]
        aim = target[part, 0]
        updated = field - ALPHA * (grad_own[part] + RHO * (field - aim))
        edge[part] = -ALPHA * grad_halo[part]
        base_out[part] = updated
        hold[part] = aim - updated
    to_right = fold(edge[0], edge[1], mask)
    to_left = fold(edge[0], edge[1], ~mask)
    to_partner[...] = jnp.where(even, to_right, to_left)
    to_other[...] = jnp.where(even, to_left, to_right)
    per_part = side // chunk
    for slab in range(slabs):
        rows = pl.ds(slab * depth, depth)
        for part in range(2):
            slabs_out[slab, part * depth : (part + 1) * depth] = hold[part, rows]
            slabs_out[slab, (2 + part) * depth : (3 + part) * depth] = edge[part, rows]
        part, place = slab // per_part, slab % per_part
        slabs_out[slab, 4 * depth : 4 * depth + chunk] = grad_probe[
            part, place * chunk : (place + 1) * chunk
        ]


def forward_kernel(slabs, turn, table, spectrum_out, rows_scratch):
    tiles, height, width = slabs.shape
    depth = rows_scratch.shape[0] // tiles
    chunk = height - 4 * depth
    mask = lane_mask((depth, width), width // 2)
    blocks = []
    for tile in range(tiles):
        block = []
        for part in range(2):
            rows = slice((2 + part) * depth, (3 + part) * depth)
            zero = jnp.zeros((depth, width), F32)
            before = slabs[tile - 1, rows] if tile > 0 else zero
            after = slabs[tile + 1, rows] if tile < tiles - 1 else zero
            block.append(
                slabs[tile, part * depth : (part + 1) * depth] - jnp.where(mask, before, after)
            )
        blocks.append(tuple(block))
    for index, (real, imag) in enumerate(butterfly(blocks, -1)):
        cosine, sine = turn[0, index : index + 1], turn[1, index : index + 1]
        rows = slice(index * depth, (index + 1) * depth)
        rows_scratch[rows, :width] = real * cosine - imag * sine
        rows_scratch[rows, width:] = real * sine + imag * cosine
    high, low = halves(rows_scratch[...])
    spectrum = dot(jnp.concatenate([high, low, high], 1), table[...])
    count = rows_scratch.shape[0]
    spectrum_out[0:count] = spectrum[:, :width]
    spectrum_out[count : 2 * count] = spectrum[:, width:]
    total = slabs[0, 4 * depth : 4 * depth + chunk]
    for tile in range(1, tiles):
        total = total + slabs[tile, 4 * depth : 4 * depth + chunk]
    spectrum_out[2 * count : 2 * count + chunk] = total


def phase_kernel(tiles, extra, table_out):
    angles, _, _, beam, width = table_out.shape
    total = tiles * width
    first = lax.axis_index("angle") * beam - (beam * lax.axis_size("angle")) // 2
    offsets = (lax.broadcasted_iota(jnp.int32, (beam, width), 0) + first).astype(F32)
    column = lax.broadcasted_iota(jnp.int32, (beam, width), 1)
    for angle in range(angles):
        shear = extra[1:2, angle : angle + 1]
        for block in range(tiles):
            frequency = block + tiles * column
            signed = jnp.where(frequency < total // 2, frequency, frequency - total).astype(F32)
            turns = (offsets * signed * shear) * (1.0 / total)
            turns = turns - jnp.floor(turns + 0.5)
            x = turns * math.pi
            square = x * x
            sine = x * (
                1.0 + square * (-1 / 6 + square * (1 / 120 + square * (-1 / 5040 + square * (
                    1 / 362880 + square * (-1 / 39916800 + square * (1.0 / 6227020800.0))))))
            )
            cosine = 1.0 + square * (-1 / 2 + square * (1 / 24 + square * (-1 / 720 + square * (
                1 / 40320 + square * (-1 / 3628800 + square * (1.0 / 479001600.0))))))
            table_out[angle, 0, block] = 1.0 - 2.0 * sine * sine
            table_out[angle, 1, block] = 2.0 * sine * cosine


def inverse_kernel(depth, spectra, phases, turn, table, image_out):
    angles, _, tiles, beam, width = phases.shape
    group = image_out.shape[1]
    wide = math.gcd(group, 2)
    first = pl.program_id(0) * group
    count = tiles * depth

    def sum_angles(start, _):
        rows = [[] for _ in range(wide)]
        for block in range(tiles):
            cosines = [phases[angle, 0, block] for angle in range(angles)]
            sines = [phases[angle, 1, block] for angle in range(angles)]
            for member in range(wide):
                real = imag = None
                for angle in range(angles):
                    at = block * depth + first + start + member
                    spec_real = spectra[angle, pl.ds(at, 1), :]
                    spec_imag = spectra[angle, pl.ds(count + at, 1), :]
                    add_real = cosines[angle] * spec_real - sines[angle] * spec_imag
                    add_imag = cosines[angle] * spec_imag + sines[angle] * spec_real
                    real = add_real if angle == 0 else real + add_real
                    imag = add_imag if angle == 0 else imag + add_imag
                rows[member].append(jnp.concatenate([real, imag], 1))
        return [halves(jnp.concatenate(blocks, 0)) for blocks in rows]

    def transform(start, splits):
        return [dot(jnp.concatenate([high, low, high], 1), table[...]) for high, low in splits]

    def finish(start, images):
        for member, image in enumerate(images):
            blocks = []
            for block in range(tiles):
                real = image[block * beam : (block + 1) * beam, :width]
                imag = image[block * beam : (block + 1) * beam, width:]
                cosine, sine = turn[0, block : block + 1], turn[1, block : block + 1]
                blocks.append((real * cosine - imag * sine, real * sine + imag * cosine))
            for index, (real, imag) in enumerate(butterfly(blocks, 1)):
                columns = slice(index * width, (index + 1) * width)
                image_out[0, start + member, :, columns] = real.astype(BF16)
                image_out[1, start + member, :, columns] = imag.astype(BF16)

    side_by_side([sum_angles, transform, finish], group, wide)


def last_kernel(probe_rows, spectra, probe, extra, base, partner, other, chunk_out, psi_out):
    angles, tiles, rows = spectra.shape[0], chunk_out.shape[0], chunk_out.shape[1]
    total = spectra[0, probe_rows : probe_rows + rows]
    for angle in range(1, angles):
        total = total + spectra[angle, probe_rows : probe_rows + rows]
    tile = lax.axis_index("tile")
    mine = probe[pl.ds(tile, 1)][0] - PROBE_STEP * total / extra[0:1]
    for place in range(tiles):
        chunk_out[place] = mine
    mask = lane_mask(base.shape[1:], base.shape[-1] // 2)
    even = is_even()
    left, right = packed_sides(partner, other, even)
    real, imag = unfold(left, right, mask)
    psi_out[0, 0] = base[0] + real
    psi_out[1, 0] = base[1] + imag


VMEM = pl.BlockSpec(memory_space=pltpu.VMEM)
SMEM = pl.BlockSpec(memory_space=pltpu.SMEM)
HBM = pl.BlockSpec(memory_space=pltpu.HBM)
ANY = pl.BlockSpec(memory_space=pl.ANY)


def call(body, name, out_shape, in_specs, scratch=(), flops=0, size=0, **more):
    return pl.pallas_call(
        body,
        name=name,
        out_shape=out_shape,
        in_specs=in_specs,
        scratch_shapes=list(scratch),
        compiler_params=pltpu.CompilerParams(vmem_limit_bytes=VMEM_LIMIT),
        cost_estimate=pl.CostEstimate(flops=flops, bytes_accessed=size, transcendentals=0),
        **more,
    )


def shape(*dims, dtype=F32):
    return jax.ShapeDtypeStruct(dims, dtype)


def exchange(to_partner, to_other, tiles):
    def pairs(start):
        low = range(start, tiles - 1, 2)
        return [(i, i + 1) for i in low] + [(i + 1, i) for i in low]

    return (
        lax.ppermute(to_partner, "tile", pairs(0)),
        lax.ppermute(to_other, "tile", pairs(1)),
    )


def swap(array, mask, devices):
    return lax.ppermute(array, ("angle", "tile"), [(i, i ^ mask) for i in range(devices)])


def hypercube(angles, tiles):
    bits = [tiles << at for at in range(1, angles.bit_length() - 1)]
    bits += [1 << at for at in range(tiles.bit_length() - 1)]
    rounds = []
    while bits:
        two, bits = bits[:2], bits[2:]
        rounds.append(two if len(two) == 1 else [two[0], two[1], two[0] ^ two[1]])
    return rounds


def shards(psi, target, probe, data, pos_z, pos_x, counts, shears):
    rows_total, width = psi.shape[2], psi.shape[3]
    side = probe.shape[1]
    angles, tiles = lax.axis_size("angle"), lax.axis_size("tile")
    devices = angles * tiles
    depth = rows_total // tiles
    beam = 32
    norm = 1.0 / math.sqrt(side)
    tables = [
        jnp.asarray(right_table(side, -1.0, norm)),
        jnp.asarray(left_table(side, -1.0, norm)),
        jnp.asarray(left_table(side, 1.0, norm)),
        jnp.asarray(right_table(side, 1.0, norm)),
    ]
    block = (2, rows_total, width)
    work = [
        pltpu.VMEM(block, F32),
        pltpu.VMEM(block, F32),
        pltpu.VMEM((2, side, side), F32),
        pltpu.VMEM((data.shape[2], 2, side, side), F32),
    ]
    slots = data.shape[2]
    flops = slots * 4 * 2 * side * 6 * side * 2 * side
    slot_places = [pltpu.with_memory_space_constraint(x, pltpu.HBM) for x in (pos_z, pos_x)]
    places = [pltpu.SMEM(x.shape, x.dtype) for x in slot_places] + [pltpu.SemaphoreType.DMA((2,))]
    psi = pltpu.with_memory_space_constraint(psi, pltpu.HBM)
    flat = shape(rows_total, width)
    to_partner, to_other = call(
        pack_kernel,
        "psi_pack",
        [flat] * 2,
        [HBM],
        [pltpu.VMEM(block, F32), pltpu.SemaphoreType.DMA((2,))],
    )(psi)
    partner, other = exchange(to_partner, to_other, tiles)
    operands = [
        pltpu.with_memory_space_constraint(x, pltpu.HBM)
        for x in [psi, target, probe, data] + tables
    ]
    psi_in, target_in, probe_in, data_in, *tables = call(
        stage_kernel,
        "stage_operands",
        [pltpu.VMEM(x.shape, x.dtype) for x in operands],
        [HBM] * len(operands),
        [pltpu.SemaphoreType.DMA((len(operands),))],
        0,
        3_000_000,
        out_specs=[VMEM] * len(operands),
    )(*operands)
    target_in, data_in, *tables = [
        pltpu.with_memory_space_constraint(x, pltpu.VMEM) for x in [target_in, data_in] + tables
    ]
    half = shape(side + 8, side)
    to_partner, to_other, base, rim, keep, send = call(
        first_kernel,
        "ptycho_first",
        [shape(*block)] * 4 + [half] * 2,
        [HBM] * 2 + [SMEM] * 2 + [VMEM] * 10,
        places + [pltpu.VMEM(block, F32)] + work,
        flops,
    )(*slot_places, counts, shears, psi_in, target_in, partner, other, probe_in, data_in, *tables)
    rounds = hypercube(angles, tiles)
    total = call(sum_kernel, "probe_sum", half, [VMEM] * 2)(keep, swap(send, tiles, devices))
    for masks in rounds[:-1]:
        terms = [total] + [swap(total, mask, devices) for mask in masks]
        total = call(sum_kernel, "probe_sum", half, [VMEM] * len(terms))(*terms)
    partner, other = exchange(to_partner, to_other, tiles)
    terms = [total] + [swap(total, mask, devices) for mask in rounds[-1]]
    probe_mine, extra = call(
        probe_kernel,
        "probe_step",
        [shape(side, side), shape(8, side)],
        [VMEM] * (1 + len(terms)),
        [pltpu.VMEM((side + 8, side), F32)],
    )(probe_in, *terms)
    probe_theirs = swap(probe_mine, tiles, devices)
    phases = call(
        functools.partial(phase_kernel, tiles),
        "phase_table",
        shape(angles, 2, tiles, beam, width),
        [VMEM],
        (),
        angles * tiles * beam * width * 40,
    )(extra)
    piece = 2 * side // tiles
    slabs, base, to_partner, to_other, probe_one = call(
        second_kernel,
        "ptycho_second",
        [shape(tiles, 4 * depth + piece, width), shape(*block), flat, flat, shape(2, side, side)],
        [HBM] * 2 + [SMEM] + [VMEM] * 12 + [ANY],
        places + [pltpu.VMEM(block, F32)] * 4 + work,
        flops,
    )(
        *(*slot_places, counts, base, rim, partner, other, target_in),
        *(probe_mine, probe_theirs, data_in, *tables, phases),
    )
    slabs = lax.all_to_all(slabs, "tile", 0, 0, tiled=True)
    partner, other = exchange(to_partner, to_other, tiles)
    count = tiles * depth
    spectrum = call(
        forward_kernel,
        "slab_spectrum",
        shape(2 * count + piece, width),
        [VMEM] * 3,
        [pltpu.VMEM((count, 2 * width), F32)],
    )(slabs, jnp.asarray(twiddles(tiles, width, -1.0, 1.0)), jnp.asarray(right_table(width, -1.0, 1.0)))
    spectra = lax.all_gather(spectrum, "angle", axis=0, tiled=False)
    chunks, psi_new = call(
        functools.partial(last_kernel, 2 * count),
        "probe_last",
        [shape(tiles, piece, side), shape(2, 1, rows_total, width)],
        [VMEM] * 6,
    )(spectra, probe_one.reshape(tiles, piece, side), extra, base, partner, other)
    probe_new = lax.all_to_all(chunks, "tile", 0, 0, tiled=True).reshape(2, side, side)
    scale = 1.0 / (angles * tiles * width)
    group = max(size for size in (1, 2, 4, 10) if depth % size == 0)
    tomo = call(
        functools.partial(inverse_kernel, depth),
        "slab_image",
        shape(2, depth, beam, tiles * width, dtype=BF16),
        [VMEM] * 4,
        [],
        depth * tiles * beam * 2 * 6 * width * 2 * width,
        grid=(depth // group,),
        out_specs=pl.BlockSpec((2, group, beam, tiles * width), lambda row: (0, row, 0, 0)),
    )(
        spectra,
        phases,
        jnp.asarray(twiddles(tiles, width, 1.0, scale)),
        jnp.asarray(right_table(width, 1.0, 1.0)),
    )
    return psi_new, probe_new, tomo


def solution(mesh):
    in_specs = (
        P(None, "angle", None, "tile"),
        P(None, "angle", None, "tile"),
        P(),
        P("angle", "tile", None, None, None),
        P("angle", "tile", None),
        P("angle", "tile", None),
        P("angle", "tile"),
        P("angle"),
    )
    out_specs = (P(None, "angle", None, "tile"), P(), P(None, "tile", "angle", None))
    return jax.shard_map(shards, mesh=mesh, in_specs=in_specs, out_specs=out_specs, check_vma=False)
```

```python
import functools
import math

import jax
import jax.numpy as jnp
import ml_dtypes
import numpy as np
from jax import lax
from jax.experimental import pallas as pl
from jax.experimental.pallas import tpu as pltpu
from jax.sharding import PartitionSpec as P

ITERS = 2
ALPHA = 0.004
RHO = 5.0
PROBE_STEP = 0.02
GROUP = 4
VMEM_LIMIT = 40 * 1024 * 1024
BF16 = jnp.bfloat16
F32 = jnp.float32


def split_table(matrix, axis):
    high = matrix.astype(ml_dtypes.bfloat16)
    low = (matrix - high.astype(np.float64)).astype(ml_dtypes.bfloat16)
    return np.concatenate([high, high, low], axis)


def dft_parts(length, orient, scale):
    counter = np.arange(length)
    angle = 2.0 * math.pi / length * (np.outer(counter, counter) % length)
    return np.cos(angle) * scale, orient * np.sin(angle) * scale


def right_table(length, orient, scale):
    real, imag = dft_parts(length, orient, scale)
    return split_table(np.block([[real, imag], [-imag, real]]), 0)


def left_table(length, orient, scale):
    real, imag = dft_parts(length, orient, scale)
    matrix = np.block([[real, -imag], [imag, real]])
    high = matrix.astype(ml_dtypes.bfloat16)
    return np.concatenate([high, (matrix - high.astype(np.float64)).astype(ml_dtypes.bfloat16)], 0)


def twiddles(tiles, inner, orient, scale):
    angle = 2.0 * math.pi / (tiles * inner) * np.outer(np.arange(tiles), np.arange(inner))
    return np.stack([np.cos(angle) * scale, orient * np.sin(angle) * scale]).astype(np.float32)


def halves(value):
    high = value.astype(BF16)
    low = (value - high.astype(F32)).astype(BF16)
    return high, low


def dot(left, right):
    return jnp.dot(left, right, preferred_element_type=F32)


def tall(table, high, low):
    size = high.shape[0]
    both = dot(table[...], high)
    return both[:size] + both[size:] + dot(table[0:size], low)


def butterfly(parts, orient):
    count = len(parts)
    if count == 1:
        return parts
    even = butterfly(parts[0::2], orient)
    odd = butterfly(parts[1::2], orient)
    low, high = [], []
    for index in range(count // 2):
        angle = orient * 2.0 * math.pi * index / count
        real, imag = odd[index]
        if index == 0:
            turned = (real, imag)
        elif 4 * index == count:
            turned = (-imag, real) if orient > 0 else (imag, -real)
        else:
            cosine, sine = math.cos(angle), math.sin(angle)
            turned = (real * cosine - imag * sine, real * sine + imag * cosine)
        base_real, base_imag = even[index]
        low.append((base_real + turned[0], base_imag + turned[1]))
        high.append((base_real - turned[0], base_imag - turned[1]))
    return low + high


def lane_mask(shape, half):
    return lax.broadcasted_iota(jnp.int32, shape, len(shape) - 1) < half


def side_by_side(stages, count, group):
    groups = count // group
    held = [None] * groups
    for turn in range(groups + len(stages) - 1):
        for number in reversed(range(len(stages))):
            at = turn - number
            if 0 <= at < groups:
                held[at] = stages[number](at * group, held[at])


def slot_loop(pos_z, pos_x, count, probe_real, probe_imag, data, tables, own, halo, work):
    right_fwd, left_fwd, left_inv, right_inv = tables
    grad_own, grad_halo, grad_probe, patches = work
    side = data.shape[-1]
    half = side // 2
    slots = data.shape[2]
    group = math.gcd(slots, GROUP)
    wide = math.gcd(group, 2)
    lanes = lax.broadcasted_iota(jnp.int32, (side, side), 1)
    grad_own[...] = jnp.zeros_like(grad_own)
    grad_halo[...] = jnp.zeros_like(grad_halo)
    grad_probe[...] = jnp.zeros_like(grad_probe)

    def place(slot):
        start = pos_x[0, 0, slot] - half
        back = jnp.where(start > 0, side - start, -start)
        forth = jnp.where(start < 0, side + start, start)
        inside = (lanes >= start) & (lanes < side + start)
        return pl.ds(pos_z[0, 0, slot], side), back, forth, inside

    def cut_out(first, _):
        waves = []
        for slot in range(first, first + group):
            where, back, _, inside = place(slot)
            cut = []
            for part in range(2):
                mixed = jnp.where(inside, own[part, where, :], halo[part, where, :])
                cut.append(pltpu.roll(mixed, back, 1))
                patches[slot, part] = cut[part]
            waves.append(
                jnp.concatenate(
                    [
                        probe_real[...] * cut[0] - probe_imag[...] * cut[1],
                        probe_real[...] * cut[1] + probe_imag[...] * cut[0],
                    ],
                    1,
                )
            )
        return halves(jnp.concatenate(waves, 0))

    def rows_forward(first, split):
        high, low = split
        rows = dot(jnp.concatenate([high, low, high], 1), right_fwd[...])
        stacks = []
        for at in range(0, group, wide):
            some = [rows[(at + k) * side : (at + k + 1) * side] for k in range(wide)]
            stacked = jnp.concatenate(
                [
                    jnp.concatenate([block[:, :side] for block in some], 1),
                    jnp.concatenate([block[:, side:] for block in some], 1),
                ],
                0,
            )
            stacks.append(halves(stacked))
        return stacks

    def columns_forward(first, stacks):
        results = []
        for index, (high, low) in enumerate(stacks):
            far = tall(left_fwd, high, low)
            weights = []
            for k in range(wide):
                slot = first + index * wide + k
                live = jnp.where(slot < count, 1.0, 0.0).astype(F32)
                far_real = far[:side, k * side : (k + 1) * side]
                far_imag = far[side:, k * side : (k + 1) * side]
                weights.append((far_real * far_real + far_imag * far_imag - data[0, 0, slot]) * live)
            weight = jnp.concatenate(weights, 1)
            results.append(halves(jnp.concatenate([far[:side] * weight, far[side:] * weight], 0)))
        return results

    def columns_inverse(first, stacks):
        blocks = []
        for high, low in stacks:
            back_cols = tall(left_inv, high, low)
            for k in range(wide):
                block = back_cols[:, k * side : (k + 1) * side]
                blocks.append(jnp.concatenate([block[:side], block[side:]], 1))
        return halves(jnp.concatenate(blocks, 0))

    def rows_inverse(first, split):
        high, low = split
        return dot(jnp.concatenate([high, low, high], 1), right_inv[...])

    def add_back(first, chi):
        sum_real, sum_imag = grad_probe[0], grad_probe[1]
        for member in range(group):
            slot = first + member
            where, _, forth, inside = place(slot)
            chi_real = chi[member * side : (member + 1) * side, :side]
            chi_imag = chi[member * side : (member + 1) * side, side:]
            cut_real, cut_imag = patches[slot, 0], patches[slot, 1]
            sum_real = sum_real + (cut_real * chi_real + cut_imag * chi_imag)
            sum_imag = sum_imag + (cut_real * chi_imag - cut_imag * chi_real)
            grads = (
                probe_real[...] * chi_real + probe_imag[...] * chi_imag,
                probe_real[...] * chi_imag - probe_imag[...] * chi_real,
            )
            for part in range(2):
                moved = pltpu.roll(grads[part], forth, 1)
                grad_own[part, where, :] += jnp.where(inside, moved, 0.0)
                grad_halo[part, where, :] += jnp.where(inside, 0.0, moved)
        grad_probe[0], grad_probe[1] = sum_real, sum_imag

    side_by_side(
        [cut_out, rows_forward, columns_forward, columns_inverse, rows_inverse, add_back], slots, group
    )


def stage_kernel(*refs):
    count = (len(refs) - 1) // 2
    copies = [
        pltpu.make_async_copy(refs[index], refs[count + index], refs[-1].at[index])
        for index in range(count)
    ]
    for copy in copies:
        copy.start()
    for copy in copies:
        copy.wait()


def sides(partner, other, part, even):
    first, second = partner[part], other[part]
    return jnp.where(even, second, first), jnp.where(even, first, second)


def is_even():
    return lax.axis_index("tile") % 2 == 0


def load_places(sources, targets, sems):
    copies = [
        pltpu.make_async_copy(source, target, sems.at[index])
        for index, (source, target) in enumerate(zip(sources, targets))
    ]
    for copy in copies:
        copy.start()
    return copies


def fold(kept, turned, mask):
    return jnp.where(mask, kept, pltpu.roll(turned, mask.shape[-1] // 2, 1))


def pack_kernel(psi, to_partner, to_other, held, sems):
    copies = [pltpu.make_async_copy(psi.at[part, 0], held.at[part], sems.at[part]) for part in range(2)]
    for copy in copies:
        copy.start()
    mask = lane_mask(to_partner.shape, to_partner.shape[-1] // 2)
    even = is_even()
    for copy in copies:
        copy.wait()
    to_left = fold(held[0], held[1], mask)
    to_right = fold(held[0], held[1], ~mask)
    to_partner[...] = jnp.where(even, to_right, to_left)
    to_other[...] = jnp.where(even, to_left, to_right)


def unfold(low_source, high_source, mask):
    real = jnp.where(mask, low_source, high_source)
    imag = pltpu.roll(jnp.where(mask, high_source, low_source), mask.shape[-1] // 2, 1)
    return real, imag


def packed_sides(partner, other, even):
    first, second = partner[...], other[...]
    return jnp.where(even, second, first), jnp.where(even, first, second)


def first_kernel(
    pos_z, pos_x, counts, shears, psi, target, partner, other, probe, data, *rest
):
    tables = rest[:4]
    to_partner, to_other, base_out, rim_out, keep_out, send_out = rest[4:10]
    held, sems, halo, work = rest[10:12], rest[12], rest[13], rest[14:]
    copies = load_places((pos_z, pos_x), held, sems)
    pos_z, pos_x = held
    grad_own, grad_halo, grad_probe = work[:3]
    side = data.shape[-1]
    mask = lane_mask(psi.shape[2:], side // 2)
    even = is_even()
    left, right = packed_sides(partner, other, even)
    halo[0], halo[1] = unfold(right, left, mask)
    for copy in copies:
        copy.wait()
    count = counts[0, 0]
    slot_loop(
        pos_z, pos_x, count, probe.at[0], probe.at[1], data, tables, psi.at[:, 0], halo, work
    )
    for part in range(2):
        field = psi[part, 0]
        base = field - ALPHA * (grad_own[part] + RHO * (field - target[part, 0]))
        rim = -ALPHA * grad_halo[part]
        base_out[part] = base
        rim_out[part] = rim
        to_right, to_left = jnp.where(mask, rim, base), jnp.where(mask, base, rim)
        to_partner[part] = jnp.where(even, to_right, to_left)
        to_other[part] = jnp.where(even, to_left, to_right)
    row = lax.broadcasted_iota(jnp.int32, (8, side), 0)
    lane = lax.broadcasted_iota(jnp.int32, (8, side), 1)
    angle, tile = lax.axis_index("angle"), lax.axis_index("tile")
    mine = (row == 1) & (lane == angle) & (tile == 0)
    extra = jnp.where(row == 0, count.astype(F32), jnp.where(mine, shears[0], 0.0))
    core = angle % 2
    for out, part in ((keep_out, core), (send_out, 1 - core)):
        out[0:side] = grad_probe[part]
        out[side : side + 8] = extra


def sum_kernel(*refs):
    terms = [ref[...] for ref in refs[:-1]]
    while len(terms) > 1:
        terms = [terms[at] + terms[at + 1] for at in range(0, len(terms), 2)]
    refs[-1][...] = terms[0]


def probe_kernel(probe, *refs):
    total, probe_out, extra_out = refs[-1], refs[-3], refs[-2]
    sum_kernel(*refs[:-3], total)
    side = probe.shape[-1]
    extra = total[side : side + 8]
    part = lax.axis_index("angle") % 2
    probe_out[...] = probe[part] - PROBE_STEP * total[0:side] / extra[0:1]
    extra_out[...] = extra


def last_probe_kernel(probe_mine, extra, *refs):
    total, probe_out = refs[-1], refs[-2]
    sum_kernel(*refs[:-2], total)
    probe_out[...] = probe_mine[...] - PROBE_STEP * total[...] / extra[0:1]


def second_kernel(
    pos_z, pos_x, counts, base, rim, partner, other, target, probe_mine, probe_theirs, data, *rest
):
    tables = rest[:4]
    slabs_out, base_out, to_partner, to_other, keep_out, send_out = rest[5:11]
    held, sems, own, halo, hold, edge, probe, work = rest[11:13], *rest[13:19], rest[19:]
    copies = load_places((pos_z, pos_x), held, sems)
    pos_z, pos_x = held
    grad_own, grad_halo, grad_probe = work[:3]
    side = data.shape[-1]
    mask = lane_mask(base.shape[1:], side // 2)
    tile, tiles = lax.axis_index("tile"), lax.axis_size("tile")
    from_right = jnp.where(tile < tiles - 1, 1.0, 0.0).astype(F32)
    from_left = jnp.where(tile > 0, 1.0, 0.0).astype(F32)
    core = lax.axis_index("angle") % 2
    probe[core] = probe_mine[...]
    probe[1 - core] = probe_theirs[...]
    even = is_even()
    for part in range(2):
        left, right = sides(partner, other, part, even)
        own[part] = base[part] + jnp.where(mask, left, right)
        halo[part] = jnp.where(
            mask, (right + rim[part]) * from_right, (left + rim[part]) * from_left
        )
    for copy in copies:
        copy.wait()
    slot_loop(
        pos_z, pos_x, counts[0, 0], probe.at[0], probe.at[1], data, tables, own, halo, work
    )
    slabs, depth = slabs_out.shape[0], base.shape[1] // slabs_out.shape[0]
    for part in range(2):
        field = own[part]
        aim = target[part, 0]
        updated = field - ALPHA * (grad_own[part] + RHO * (field - aim))
        edge[part] = -ALPHA * grad_halo[part]
        base_out[part] = updated
        hold[part] = aim - updated
    to_right = fold(edge[0], edge[1], mask)
    to_left = fold(edge[0], edge[1], ~mask)
    to_partner[...] = jnp.where(even, to_right, to_left)
    to_other[...] = jnp.where(even, to_left, to_right)
    keep_out[...] = grad_probe[core]
    send_out[...] = grad_probe[1 - core]
    for slab in range(slabs):
        rows = pl.ds(slab * depth, depth)
        for part in range(2):
            slabs_out[slab, part * depth : (part + 1) * depth] = hold[part, rows]
            slabs_out[slab, (2 + part) * depth : (3 + part) * depth] = edge[part, rows]


def forward_kernel(slabs, turn, table, *rest):
    spectrum_out, rows_scratch = rest[-2:]
    tiles, _, width = slabs.shape
    depth = rows_scratch.shape[0] // tiles
    mask = lane_mask((depth, width), width // 2)
    blocks = []
    for tile in range(tiles):
        block = []
        for part in range(2):
            rows = slice((2 + part) * depth, (3 + part) * depth)
            zero = jnp.zeros((depth, width), F32)
            before = slabs[tile - 1, rows] if tile > 0 else zero
            after = slabs[tile + 1, rows] if tile < tiles - 1 else zero
            block.append(
                slabs[tile, part * depth : (part + 1) * depth] - jnp.where(mask, before, after)
            )
        blocks.append(tuple(block))
    for index, (real, imag) in enumerate(butterfly(blocks, -1)):
        cosine, sine = turn[0, index : index + 1], turn[1, index : index + 1]
        rows = slice(index * depth, (index + 1) * depth)
        rows_scratch[rows, :width] = real * cosine - imag * sine
        rows_scratch[rows, width:] = real * sine + imag * cosine
    high, low = halves(rows_scratch[...])
    spectrum = dot(jnp.concatenate([high, low, high], 1), table[...])
    count = rows_scratch.shape[0]
    spectrum_out[0:count] = spectrum[:, :width]
    spectrum_out[count : 2 * count] = spectrum[:, width:]


def phase_kernel(tiles, extra, table_out):
    angles, _, _, beam, width = table_out.shape
    total = tiles * width
    first = lax.axis_index("angle") * beam - (beam * lax.axis_size("angle")) // 2
    offsets = (lax.broadcasted_iota(jnp.int32, (beam, width), 0) + first).astype(F32)
    column = lax.broadcasted_iota(jnp.int32, (beam, width), 1)
    for angle in range(angles):
        shear = extra[1:2, angle : angle + 1]
        for block in range(tiles):
            frequency = block + tiles * column
            signed = jnp.where(frequency < total // 2, frequency, frequency - total).astype(F32)
            turns = (offsets * signed * shear) * (1.0 / total)
            turns = turns - jnp.floor(turns + 0.5)
            x = turns * math.pi
            square = x * x
            sine = x * (
                1.0 + square * (-1 / 6 + square * (1 / 120 + square * (-1 / 5040 + square * (
                    1 / 362880 + square * (-1 / 39916800 + square * (1.0 / 6227020800.0))))))
            )
            cosine = 1.0 + square * (-1 / 2 + square * (1 / 24 + square * (-1 / 720 + square * (
                1 / 40320 + square * (-1 / 3628800 + square * (1.0 / 479001600.0))))))
            table_out[angle, 0, block] = 1.0 - 2.0 * sine * sine
            table_out[angle, 1, block] = 2.0 * sine * cosine


def inverse_kernel(depth, masks, phases, turn, table, *rest):
    spectra, image_out, token = rest[: len(masks)], rest[-2], rest[-1]
    token[...] = jnp.zeros_like(token)
    _, _, tiles, beam, width = phases.shape
    angles = [lax.axis_index("angle") ^ mask for mask in masks]
    group = image_out.shape[1]
    wide = math.gcd(group, 2)
    first = pl.program_id(0) * group
    count = tiles * depth

    def sum_angles(start, _):
        rows = [[] for _ in range(wide)]
        for block in range(tiles):
            cosines = [phases[angle, 0, block] for angle in angles]
            sines = [phases[angle, 1, block] for angle in angles]
            for member in range(wide):
                real = imag = None
                for spectrum, cosine, sine in zip(spectra, cosines, sines):
                    at = block * depth + first + start + member
                    spec_real = spectrum[pl.ds(at, 1), :]
                    spec_imag = spectrum[pl.ds(count + at, 1), :]
                    add_real = cosine * spec_real - sine * spec_imag
                    add_imag = cosine * spec_imag + sine * spec_real
                    real = add_real if real is None else real + add_real
                    imag = add_imag if imag is None else imag + add_imag
                rows[member].append(jnp.concatenate([real, imag], 1))
        return [halves(jnp.concatenate(blocks, 0)) for blocks in rows]

    def transform(start, splits):
        return [dot(jnp.concatenate([high, low, high], 1), table[...]) for high, low in splits]

    def finish(start, images):
        for member, image in enumerate(images):
            blocks = []
            for block in range(tiles):
                real = image[block * beam : (block + 1) * beam, :width]
                imag = image[block * beam : (block + 1) * beam, width:]
                cosine, sine = turn[0, block : block + 1], turn[1, block : block + 1]
                blocks.append((real * cosine - imag * sine, real * sine + imag * cosine))
            for index, (real, imag) in enumerate(butterfly(blocks, 1)):
                columns = slice(index * width, (index + 1) * width)
                image_out[0, start + member, :, columns] = real.astype(BF16)
                image_out[1, start + member, :, columns] = imag.astype(BF16)

    side_by_side([sum_angles, transform, finish], group, wide)


def finish_kernel(base, partner, other, probe_mine, probe_theirs, _, psi_out, probe_out):
    mask = lane_mask(base.shape[1:], base.shape[-1] // 2)
    left, right = packed_sides(partner, other, is_even())
    real, imag = unfold(left, right, mask)
    psi_out[0, 0] = base[0] + real
    psi_out[1, 0] = base[1] + imag
    core = lax.axis_index("angle") % 2
    probe_out[core] = probe_mine[...]
    probe_out[1 - core] = probe_theirs[...]


VMEM = pl.BlockSpec(memory_space=pltpu.VMEM)
SMEM = pl.BlockSpec(memory_space=pltpu.SMEM)
HBM = pl.BlockSpec(memory_space=pltpu.HBM)
ANY = pl.BlockSpec(memory_space=pl.ANY)


def call(body, name, out_shape, in_specs, scratch=(), flops=0, size=0, **more):
    return pl.pallas_call(
        body,
        name=name,
        out_shape=out_shape,
        in_specs=in_specs,
        scratch_shapes=list(scratch),
        compiler_params=pltpu.CompilerParams(vmem_limit_bytes=VMEM_LIMIT),
        cost_estimate=pl.CostEstimate(flops=flops, bytes_accessed=size, transcendentals=0),
        **more,
    )


def shape(*dims, dtype=F32):
    return jax.ShapeDtypeStruct(dims, dtype)


def exchange(to_partner, to_other, tiles):
    def pairs(start):
        low = range(start, tiles - 1, 2)
        return [(i, i + 1) for i in low] + [(i + 1, i) for i in low]

    return (
        lax.ppermute(to_partner, "tile", pairs(0)),
        lax.ppermute(to_other, "tile", pairs(1)),
    )


def swap(array, mask, devices):
    return lax.ppermute(array, ("angle", "tile"), [(i, i ^ mask) for i in range(devices)])


def hypercube(angles, tiles):
    bits = [tiles << at for at in range(1, angles.bit_length() - 1)]
    bits += [1 << at for at in range(tiles.bit_length() - 1)]
    rounds = []
    while bits:
        two, bits = bits[:2], bits[2:]
        rounds.append(two if len(two) == 1 else [two[0], two[1], two[0] ^ two[1]])
    return rounds


def shards(psi, target, probe, data, pos_z, pos_x, counts, shears):
    rows_total, width = psi.shape[2], psi.shape[3]
    side = probe.shape[1]
    angles, tiles = lax.axis_size("angle"), lax.axis_size("tile")
    devices = angles * tiles
    depth = rows_total // tiles
    beam = 32
    norm = 1.0 / math.sqrt(side)
    tables = [
        jnp.asarray(right_table(side, -1.0, norm)),
        jnp.asarray(left_table(side, -1.0, norm)),
        jnp.asarray(left_table(side, 1.0, norm)),
        jnp.asarray(right_table(side, 1.0, norm)),
    ]
    block = (2, rows_total, width)
    work = [
        pltpu.VMEM(block, F32),
        pltpu.VMEM(block, F32),
        pltpu.VMEM((2, side, side), F32),
        pltpu.VMEM((data.shape[2], 2, side, side), F32),
    ]
    slots = data.shape[2]
    flops = slots * 4 * 2 * side * 6 * side * 2 * side
    slot_places = [pltpu.with_memory_space_constraint(x, pltpu.HBM) for x in (pos_z, pos_x)]
    places = [pltpu.SMEM(x.shape, x.dtype) for x in slot_places] + [pltpu.SemaphoreType.DMA((2,))]
    psi = pltpu.with_memory_space_constraint(psi, pltpu.HBM)
    flat = shape(rows_total, width)
    to_partner, to_other = call(
        pack_kernel,
        "psi_pack",
        [flat] * 2,
        [HBM],
        [pltpu.VMEM(block, F32), pltpu.SemaphoreType.DMA((2,))],
    )(psi)
    partner, other = exchange(to_partner, to_other, tiles)
    operands = [
        pltpu.with_memory_space_constraint(x, pltpu.HBM)
        for x in [psi, target, probe, data] + tables
    ]
    psi_in, target_in, probe_in, data_in, *tables = call(
        stage_kernel,
        "stage_operands",
        [pltpu.VMEM(x.shape, x.dtype) for x in operands],
        [HBM] * len(operands),
        [pltpu.SemaphoreType.DMA((len(operands),))],
        0,
        3_000_000,
        out_specs=[VMEM] * len(operands),
    )(*operands)
    target_in, data_in, *tables = [
        pltpu.with_memory_space_constraint(x, pltpu.VMEM) for x in [target_in, data_in] + tables
    ]
    half = shape(side + 8, side)
    to_partner, to_other, base, rim, keep, send = call(
        first_kernel,
        "ptycho_first",
        [shape(*block)] * 4 + [half] * 2,
        [HBM] * 2 + [SMEM] * 2 + [VMEM] * 10,
        places + [pltpu.VMEM(block, F32)] + work,
        flops,
    )(*slot_places, counts, shears, psi_in, target_in, partner, other, probe_in, data_in, *tables)
    rounds = hypercube(angles, tiles)

    def all_but_last(keep, send, rounds):
        piece = shape(*keep.shape)
        total = call(sum_kernel, "probe_sum", piece, [VMEM] * 2)(keep, swap(send, tiles, devices))
        for masks in rounds[:-1]:
            terms = [total] + [swap(total, mask, devices) for mask in masks]
            total = call(sum_kernel, "probe_sum", piece, [VMEM] * len(terms))(*terms)
        return total

    def last_round(total, rounds):
        return [total] + [swap(total, mask, devices) for mask in rounds[-1]]

    terms = last_round(all_but_last(keep, send, rounds), rounds)
    partner, other = exchange(to_partner, to_other, tiles)
    probe_mine, extra = call(
        probe_kernel,
        "probe_step",
        [shape(side, side), shape(8, side)],
        [VMEM] * (1 + len(terms)),
        [pltpu.VMEM((side + 8, side), F32)],
    )(probe_in, *terms)
    probe_theirs = swap(probe_mine, tiles, devices)
    phases = call(
        functools.partial(phase_kernel, tiles),
        "phase_table",
        shape(angles, 2, tiles, beam, width),
        [VMEM],
        (),
        angles * tiles * beam * width * 40,
    )(extra)
    slabs, base, to_partner, to_other, keep, send = call(
        second_kernel,
        "ptycho_second",
        [shape(tiles, 4 * depth, width), shape(*block), flat, flat] + [shape(side, side)] * 2,
        [HBM] * 2 + [SMEM] + [VMEM] * 12 + [ANY],
        places + [pltpu.VMEM(block, F32)] * 4 + [pltpu.VMEM((2, side, side), F32)] + work,
        flops,
    )(
        *(*slot_places, counts, base, rim, partner, other, target_in),
        *(probe_mine, probe_theirs, data_in, *tables, phases),
    )
    slabs = lax.all_to_all(slabs, "tile", 0, 0, tiled=True)
    total = all_but_last(keep, send, rounds)
    late = total
    for mask in rounds[-1][: 1 if len(rounds[-1]) > 1 else 0]:
        late = call(sum_kernel, "probe_sum", shape(*late.shape), [VMEM] * 2)(
            late, swap(late, mask, devices)
        )
    count = tiles * depth
    spectrum = call(
        forward_kernel,
        "slab_spectrum",
        shape(2 * count, width),
        [VMEM] * 3 + [ANY],
        [pltpu.VMEM((count, 2 * width), F32)],
    )(
        slabs,
        jnp.asarray(twiddles(tiles, width, -1.0, 1.0)),
        jnp.asarray(right_table(width, -1.0, 1.0)),
        total,
    )
    masks = list(range(angles))
    spectra = [spectrum] + [swap(spectrum, mask * tiles, devices) for mask in masks[1:]]
    late, spectra[1], to_partner, to_other = lax.optimization_barrier(
        (late, spectra[1], to_partner, to_other)
    )
    terms = [late, swap(late, rounds[-1][min(1, len(rounds[-1]) - 1)], devices)]
    partner, other = exchange(to_partner, to_other, tiles)
    probe_mine = call(
        last_probe_kernel,
        "probe_last",
        shape(side, side),
        [VMEM] * (2 + len(terms)),
        [pltpu.VMEM((side, side), F32)],
    )(probe_mine, extra, *terms)
    probe_theirs = swap(probe_mine, tiles, devices)
    scale = 1.0 / (angles * tiles * width)
    group = max(size for size in (1, 2, 4, 10) if depth % size == 0)
    tomo, token = call(
        functools.partial(inverse_kernel, depth, masks),
        "slab_image",
        [shape(2, depth, beam, tiles * width, dtype=BF16), shape(8, width)],
        [VMEM] * (3 + angles) + [ANY],
        [],
        depth * tiles * beam * 2 * 6 * width * 2 * width,
        grid=(depth // group,),
        out_specs=[
            pl.BlockSpec((2, group, beam, tiles * width), lambda row: (0, row, 0, 0)),
            pl.BlockSpec((8, width), lambda row: (0, 0)),
        ],
    )(
        phases,
        jnp.asarray(twiddles(tiles, width, 1.0, scale)),
        jnp.asarray(right_table(width, 1.0, 1.0)),
        *spectra,
        probe_mine,
    )
    psi_new, probe_new = call(
        finish_kernel,
        "field_probe",
        [shape(2, 1, rows_total, width), shape(2, side, side)],
        [VMEM] * 5 + [ANY],
    )(base, partner, other, probe_mine, probe_theirs, token)
    return psi_new, probe_new, tomo


def solution(mesh):
    in_specs = (
        P(None, "angle", None, "tile"),
        P(None, "angle", None, "tile"),
        P(),
        P("angle", "tile", None, None, None),
        P("angle", "tile", None),
        P("angle", "tile", None),
        P("angle", "tile"),
        P("angle"),
    )
    out_specs = (P(None, "angle", None, "tile"), P(), P(None, "tile", "angle", None))
    return jax.shard_map(shards, mesh=mesh, in_specs=in_specs, out_specs=out_specs, check_vma=False)
```

```python
import functools
import math

import jax
import jax.numpy as jnp
import ml_dtypes
import numpy as np
from jax import lax
from jax.experimental import pallas as pl
from jax.experimental.pallas import tpu as pltpu
from jax.sharding import PartitionSpec as P

ITERS = 2
ALPHA = 0.004
RHO = 5.0
PROBE_STEP = 0.02
GROUP = 4
VMEM_LIMIT = 40 * 1024 * 1024
BF16 = jnp.bfloat16
F32 = jnp.float32


def split_table(matrix, axis):
    high = matrix.astype(ml_dtypes.bfloat16)
    low = (matrix - high.astype(np.float64)).astype(ml_dtypes.bfloat16)
    return np.concatenate([high, high, low], axis)


def dft_parts(length, orient, scale):
    counter = np.arange(length)
    angle = 2.0 * math.pi / length * (np.outer(counter, counter) % length)
    return np.cos(angle) * scale, orient * np.sin(angle) * scale


def right_table(length, orient, scale):
    real, imag = dft_parts(length, orient, scale)
    return split_table(np.block([[real, imag], [-imag, real]]), 0)


def left_table(length, orient, scale):
    real, imag = dft_parts(length, orient, scale)
    matrix = np.block([[real, -imag], [imag, real]])
    high = matrix.astype(ml_dtypes.bfloat16)
    return np.concatenate([high, (matrix - high.astype(np.float64)).astype(ml_dtypes.bfloat16)], 0)


def twiddles(tiles, inner, orient, scale):
    angle = 2.0 * math.pi / (tiles * inner) * np.outer(np.arange(tiles), np.arange(inner))
    return np.stack([np.cos(angle) * scale, orient * np.sin(angle) * scale]).astype(np.float32)


def halves(value):
    high = value.astype(BF16)
    low = (value - high.astype(F32)).astype(BF16)
    return high, low


def dot(left, right):
    return jnp.dot(left, right, preferred_element_type=F32)


def tall(table, high, low):
    size = high.shape[0]
    both = dot(table[...], high)
    return both[:size] + both[size:] + dot(table[0:size], low)


def butterfly(parts, orient):
    count = len(parts)
    if count == 1:
        return parts
    even = butterfly(parts[0::2], orient)
    odd = butterfly(parts[1::2], orient)
    low, high = [], []
    for index in range(count // 2):
        angle = orient * 2.0 * math.pi * index / count
        real, imag = odd[index]
        if index == 0:
            turned = (real, imag)
        elif 4 * index == count:
            turned = (-imag, real) if orient > 0 else (imag, -real)
        elif 8 * index in (count, 3 * count):
            tangent = orient if 8 * index == count else -orient
            plus, minus = (real + imag, imag - real)
            turned = (-minus, plus) if tangent > 0 else (plus, minus)
            turned = tuple(math.cos(angle) * value for value in turned)
        else:
            cosine, sine = math.cos(angle), math.sin(angle)
            turned = (real * cosine - imag * sine, real * sine + imag * cosine)
        base_real, base_imag = even[index]
        low.append((base_real + turned[0], base_imag + turned[1]))
        high.append((base_real - turned[0], base_imag - turned[1]))
    return low + high


def lane_mask(shape, half):
    return lax.broadcasted_iota(jnp.int32, shape, len(shape) - 1) < half


def side_by_side(stages, count, group):
    groups = count // group
    held = [None] * groups
    for turn in range(groups + len(stages) - 1):
        for number in reversed(range(len(stages))):
            at = turn - number
            if 0 <= at < groups:
                held[at] = stages[number](at * group, held[at])


def slot_loop(pos_z, pos_x, count, probe_real, probe_imag, data, tables, own, halo, work):
    right_fwd, left_fwd, left_inv, right_inv = tables
    grad_own, grad_halo, grad_probe, patches = work
    side = data.shape[-1]
    half = side // 2
    slots = data.shape[2]
    group = math.gcd(slots, GROUP)
    wide = math.gcd(group, 2)
    lanes = lax.broadcasted_iota(jnp.int32, (8, side), 1)
    grad_own[...] = jnp.zeros_like(grad_own)
    grad_halo[...] = jnp.zeros_like(grad_halo)
    grad_probe[...] = jnp.zeros_like(grad_probe)

    def place(slot):
        start = pos_x[0, 0, slot] - half
        back = jnp.where(start > 0, side - start, -start)
        forth = jnp.where(start < 0, side + start, start)
        inside = (lanes >= start) & (lanes < side + start)
        return pl.ds(pos_z[0, 0, slot], side), back, forth, inside

    def pick(inside, yes, no):
        rows = (side // 8, 8, side)
        return jnp.where(inside[None], yes.reshape(rows), no.reshape(rows)).reshape(side, side)

    def cut_out(first, _):
        waves = []
        for slot in range(first, first + group):
            where, back, _, inside = place(slot)
            cut = []
            for part in range(2):
                mixed = pick(inside, own[part, where, :], halo[part, where, :])
                cut.append(pltpu.roll(mixed, back, 1))
                patches[slot, part] = cut[part]
            waves.append(
                jnp.concatenate(
                    [
                        probe_real[...] * cut[0] - probe_imag[...] * cut[1],
                        probe_real[...] * cut[1] + probe_imag[...] * cut[0],
                    ],
                    1,
                )
            )
        return halves(jnp.concatenate(waves, 0))

    def rows_forward(first, split):
        high, low = split
        rows = dot(jnp.concatenate([high, low, high], 1), right_fwd[...])
        stacks = []
        for at in range(0, group, wide):
            some = [rows[(at + k) * side : (at + k + 1) * side] for k in range(wide)]
            stacked = jnp.concatenate(
                [
                    jnp.concatenate([block[:, :side] for block in some], 1),
                    jnp.concatenate([block[:, side:] for block in some], 1),
                ],
                0,
            )
            stacks.append(halves(stacked))
        return stacks

    def columns_forward(first, stacks):
        results = []
        for index, (high, low) in enumerate(stacks):
            far = tall(left_fwd, high, low)
            weights = []
            for k in range(wide):
                slot = first + index * wide + k
                live = jnp.where(slot < count, 1.0, 0.0).astype(F32)
                far_real = far[:side, k * side : (k + 1) * side]
                far_imag = far[side:, k * side : (k + 1) * side]
                weights.append((far_real * far_real + far_imag * far_imag - data[0, 0, slot]) * live)
            weight = jnp.concatenate(weights, 1)
            results.append(halves(jnp.concatenate([far[:side] * weight, far[side:] * weight], 0)))
        return results

    def columns_inverse(first, stacks):
        blocks = []
        for high, low in stacks:
            back_cols = tall(left_inv, high, low)
            for k in range(wide):
                block = back_cols[:, k * side : (k + 1) * side]
                blocks.append(jnp.concatenate([block[:side], block[side:]], 1))
        return halves(jnp.concatenate(blocks, 0))

    def rows_inverse(first, split):
        high, low = split
        return dot(jnp.concatenate([high, low, high], 1), right_inv[...])

    def add_back(first, chi):
        sum_real, sum_imag = grad_probe[0], grad_probe[1]
        for member in range(group):
            slot = first + member
            where, _, forth, inside = place(slot)
            chi_real = chi[member * side : (member + 1) * side, :side]
            chi_imag = chi[member * side : (member + 1) * side, side:]
            cut_real, cut_imag = patches[slot, 0], patches[slot, 1]
            sum_real = sum_real + (cut_real * chi_real + cut_imag * chi_imag)
            sum_imag = sum_imag + (cut_real * chi_imag - cut_imag * chi_real)
            grads = (
                probe_real[...] * chi_real + probe_imag[...] * chi_imag,
                probe_real[...] * chi_imag - probe_imag[...] * chi_real,
            )
            for part in range(2):
                moved = pltpu.roll(grads[part], forth, 1)
                zero = jnp.zeros_like(moved)
                grad_own[part, where, :] += pick(inside, moved, zero)
                grad_halo[part, where, :] += pick(inside, zero, moved)
        grad_probe[0], grad_probe[1] = sum_real, sum_imag

    side_by_side(
        [cut_out, rows_forward, columns_forward, columns_inverse, rows_inverse, add_back], slots, group
    )


def stage_kernel(*refs):
    count = (len(refs) - 1) // 2
    copies = [
        pltpu.make_async_copy(refs[index], refs[count + index], refs[-1].at[index])
        for index in range(count)
    ]
    for copy in copies:
        copy.start()
    for copy in copies:
        copy.wait()


def sides(partner, other, part, even):
    first, second = partner[part], other[part]
    return jnp.where(even, second, first), jnp.where(even, first, second)


def is_even():
    return lax.axis_index("tile") % 2 == 0


def load_places(sources, targets, sems):
    copies = [
        pltpu.make_async_copy(source, target, sems.at[index])
        for index, (source, target) in enumerate(zip(sources, targets))
    ]
    for copy in copies:
        copy.start()
    return copies


def fold(kept, turned, mask):
    return jnp.where(mask, kept, pltpu.roll(turned, mask.shape[-1] // 2, 1))


def pack_kernel(psi, to_partner, to_other, held, sems):
    copies = [pltpu.make_async_copy(psi.at[part, 0], held.at[part], sems.at[part]) for part in range(2)]
    for copy in copies:
        copy.start()
    mask = lane_mask(to_partner.shape, to_partner.shape[-1] // 2)
    even = is_even()
    for copy in copies:
        copy.wait()
    to_left = fold(held[0], held[1], mask)
    to_right = fold(held[0], held[1], ~mask)
    to_partner[...] = jnp.where(even, to_right, to_left)
    to_other[...] = jnp.where(even, to_left, to_right)


def unfold(low_source, high_source, mask):
    real = jnp.where(mask, low_source, high_source)
    imag = pltpu.roll(jnp.where(mask, high_source, low_source), mask.shape[-1] // 2, 1)
    return real, imag


def packed_sides(partner, other, even):
    first, second = partner[...], other[...]
    return jnp.where(even, second, first), jnp.where(even, first, second)


def first_kernel(
    pos_z, pos_x, counts, shears, psi, target, partner, other, probe, data, *rest
):
    tables = rest[:4]
    to_partner, to_other, base_out, rim_out, keep_out, send_out = rest[4:10]
    held, sems, halo, work = rest[10:12], rest[12], rest[13], rest[14:]
    copies = load_places((pos_z, pos_x), held, sems)
    pos_z, pos_x = held
    grad_own, grad_halo, grad_probe = work[:3]
    side = data.shape[-1]
    mask = lane_mask(psi.shape[2:], side // 2)
    even = is_even()
    left, right = packed_sides(partner, other, even)
    halo[0], halo[1] = unfold(right, left, mask)
    for copy in copies:
        copy.wait()
    count = counts[0, 0]
    slot_loop(
        pos_z, pos_x, count, probe.at[0], probe.at[1], data, tables, psi.at[:, 0], halo, work
    )
    for part in range(2):
        field = psi[part, 0]
        base = field - ALPHA * (grad_own[part] + RHO * (field - target[part, 0]))
        rim = -ALPHA * grad_halo[part]
        base_out[part] = base
        rim_out[part] = rim
        to_right, to_left = jnp.where(mask, rim, base), jnp.where(mask, base, rim)
        to_partner[part] = jnp.where(even, to_right, to_left)
        to_other[part] = jnp.where(even, to_left, to_right)
    row = lax.broadcasted_iota(jnp.int32, (8, side), 0)
    lane = lax.broadcasted_iota(jnp.int32, (8, side), 1)
    angle, tile = lax.axis_index("angle"), lax.axis_index("tile")
    mine = (row == 1) & (lane == angle) & (tile == 0)
    extra = jnp.where(row == 0, count.astype(F32), jnp.where(mine, shears[0], 0.0))
    core = angle % 2
    for out, part in ((keep_out, core), (send_out, 1 - core)):
        out[0:side] = grad_probe[part]
        out[side : side + 8] = extra


def sum_kernel(*refs):
    terms = [ref[...] for ref in refs[:-1]]
    while len(terms) > 1:
        terms = [terms[at] + terms[at + 1] for at in range(0, len(terms), 2)]
    refs[-1][...] = terms[0]


def probe_kernel(probe, *refs):
    total, probe_out, extra_out = refs[-1], refs[-3], refs[-2]
    sum_kernel(*refs[:-3], total)
    side = probe.shape[-1]
    extra = total[side : side + 8]
    part = lax.axis_index("angle") % 2
    probe_out[...] = probe[part] - PROBE_STEP * total[0:side] / extra[0:1]
    extra_out[...] = extra


def last_probe_kernel(probe_mine, extra, *refs):
    total, probe_out = refs[-1], refs[-2]
    sum_kernel(*refs[:-2], total)
    probe_out[...] = probe_mine[...] - PROBE_STEP * total[...] / extra[0:1]


def second_kernel(
    pos_z, pos_x, counts, base, rim, partner, other, target, probe_mine, probe_theirs, data, *rest
):
    tables = rest[:4]
    base_out, to_partner, to_other, keep_out, send_out = rest[5:10]
    inner = inner_count(lax.axis_size("tile"))
    slab_outs, rest = rest[10 : 10 + inner], rest[10 + inner :]
    held, sems, own, halo, hold, edge, probe, work = rest[:2], *rest[2:8], rest[8:]
    copies = load_places((pos_z, pos_x), held, sems)
    pos_z, pos_x = held
    grad_own, grad_halo, grad_probe = work[:3]
    side = data.shape[-1]
    mask = lane_mask(base.shape[1:], side // 2)
    tile, tiles = lax.axis_index("tile"), lax.axis_size("tile")
    from_right = jnp.where(tile < tiles - 1, 1.0, 0.0).astype(F32)
    from_left = jnp.where(tile > 0, 1.0, 0.0).astype(F32)
    core = lax.axis_index("angle") % 2
    probe[core] = probe_mine[...]
    probe[1 - core] = probe_theirs[...]
    even = is_even()
    for part in range(2):
        left, right = sides(partner, other, part, even)
        own[part] = base[part] + jnp.where(mask, left, right)
        halo[part] = jnp.where(
            mask, (right + rim[part]) * from_right, (left + rim[part]) * from_left
        )
    for copy in copies:
        copy.wait()
    slot_loop(
        pos_z, pos_x, counts[0, 0], probe.at[0], probe.at[1], data, tables, own, halo, work
    )
    for part in range(2):
        field = own[part]
        aim = target[part, 0]
        updated = field - ALPHA * (grad_own[part] + RHO * (field - aim))
        edge[part] = -ALPHA * grad_halo[part]
        base_out[part] = updated
        hold[part] = aim - updated
    to_right = fold(edge[0], edge[1], mask)
    to_left = fold(edge[0], edge[1], ~mask)
    to_partner[...] = jnp.where(even, to_right, to_left)
    to_other[...] = jnp.where(even, to_left, to_right)
    keep_out[...] = grad_probe[core]
    send_out[...] = grad_probe[1 - core]
    outer, depth = slab_outs[0].shape[0], slab_outs[0].shape[1] // 4
    for step, slab_out in enumerate(slab_outs):
        for place in range(outer):
            slab = place * inner + ((tile % inner) ^ step)
            rows = pl.ds(slab * depth, depth)
            for part in range(2):
                slab_out[place, part * depth : (part + 1) * depth] = hold[part, rows]
                slab_out[place, (2 + part) * depth : (3 + part) * depth] = edge[part, rows]


def merge_kernel(*refs):
    tile = lax.axis_index("tile")
    inner = inner_count(lax.axis_size("tile"))
    arrived, merged = refs[:inner], refs[inner:]
    for step, source in enumerate(arrived):
        for mask, out in enumerate(merged):
            out[(tile % inner) ^ step] = source[(tile // inner) ^ mask]


def forward_kernel(turn, table, _, *rest):
    *arrived, spectrum_out, rows_scratch, slabs = rest
    inner, _, width = arrived[0].shape
    tiles = slabs.shape[0]
    depth = rows_scratch.shape[0] // tiles
    outer = lax.axis_index("tile") // inner
    for mask, source in enumerate(arrived):
        slabs[pl.ds((outer ^ mask) * inner, inner)] = source[...]
    mask = lane_mask((depth, width), width // 2)
    blocks = []
    for tile in range(tiles):
        block = []
        for part in range(2):
            rows = slice((2 + part) * depth, (3 + part) * depth)
            zero = jnp.zeros((depth, width), F32)
            before = slabs[tile - 1, rows] if tile > 0 else zero
            after = slabs[tile + 1, rows] if tile < tiles - 1 else zero
            block.append(
                slabs[tile, part * depth : (part + 1) * depth] - jnp.where(mask, before, after)
            )
        blocks.append(tuple(block))
    for index, (real, imag) in enumerate(butterfly(blocks, -1)):
        cosine, sine = turn[0, index : index + 1], turn[1, index : index + 1]
        rows = slice(index * depth, (index + 1) * depth)
        rows_scratch[rows, :width] = real * cosine - imag * sine
        rows_scratch[rows, width:] = real * sine + imag * cosine
    high, low = halves(rows_scratch[...])
    spectrum = dot(jnp.concatenate([high, low, high], 1), table[...])
    count = rows_scratch.shape[0]
    spectrum_out[0:count] = spectrum[:, :width]
    spectrum_out[count : 2 * count] = spectrum[:, width:]


def phase_kernel(tiles, extra, table_out):
    angles, _, _, beam, width = table_out.shape
    total = tiles * width
    first = lax.axis_index("angle") * beam - (beam * lax.axis_size("angle")) // 2
    offsets = (lax.broadcasted_iota(jnp.int32, (beam, width), 0) + first).astype(F32)
    column = lax.broadcasted_iota(jnp.int32, (beam, width), 1)
    for angle in range(angles):
        shear = extra[1:2, angle : angle + 1]
        for block in range(tiles):
            frequency = block + tiles * column
            signed = jnp.where(frequency < total // 2, frequency, frequency - total).astype(F32)
            turns = (offsets * signed * shear) * (1.0 / total)
            turns = turns - jnp.floor(turns + 0.5)
            x = turns * math.pi
            square = x * x
            sine = x * (
                1.0 + square * (-1 / 6 + square * (1 / 120 + square * (-1 / 5040 + square * (
                    1 / 362880 + square * (-1 / 39916800 + square * (1.0 / 6227020800.0))))))
            )
            cosine = 1.0 + square * (-1 / 2 + square * (1 / 24 + square * (-1 / 720 + square * (
                1 / 40320 + square * (-1 / 3628800 + square * (1.0 / 479001600.0))))))
            real = 1.0 - 2.0 * sine * sine
            imag = 2.0 * sine * cosine
            table_out[angle, 0, block] = real
            table_out[angle, 1, block] = imag - real
            table_out[angle, 2, block] = real + imag


def inverse_kernel(depth, masks, phases, turn, table, *rest):
    spectra = rest[: len(masks)]
    last, (image_out, psi_out, probe_out) = rest[len(masks) : -3], rest[-3:]
    _, _, tiles, beam, width = phases.shape
    angles = [lax.axis_index("angle") ^ mask for mask in masks]
    group = image_out.shape[1]

    @pl.when(pl.program_id(0) == 0)
    def _():
        finish(*last, psi_out, probe_out)

    wide = math.gcd(group, 2)
    first = pl.program_id(0) * group
    count = tiles * depth

    def sum_angles(start, _):
        rows = [[] for _ in range(wide)]
        for block in range(tiles):
            tables = [[phases[angle, which, block] for which in range(3)] for angle in angles]
            for member in range(wide):
                at = block * depth + first + start + member
                sums = None
                for spectrum, three in zip(spectra, tables):
                    real = spectrum[pl.ds(at, 1), :]
                    imag = spectrum[pl.ds(count + at, 1), :]
                    terms = [factor * one for factor, one in zip((real + imag, real, imag), three)]
                    sums = terms if sums is None else [x + y for x, y in zip(sums, terms)]
                rows[member].append(jnp.concatenate([sums[0] - sums[2], sums[0] + sums[1]], 1))
        return [halves(jnp.concatenate(blocks, 0)) for blocks in rows]

    def transform(start, splits):
        return [dot(jnp.concatenate([high, low, high], 1), table[...]) for high, low in splits]

    def store(start, images):
        for member, image in enumerate(images):
            blocks = []
            for block in range(tiles):
                real = image[block * beam : (block + 1) * beam, :width]
                imag = image[block * beam : (block + 1) * beam, width:]
                cosine, sine = turn[0, block : block + 1], turn[1, block : block + 1]
                blocks.append((real * cosine - imag * sine, real * sine + imag * cosine))
            for index, (real, imag) in enumerate(butterfly(blocks, 1)):
                columns = slice(index * width, (index + 1) * width)
                image_out[0, start + member, :, columns] = real.astype(BF16)
                image_out[1, start + member, :, columns] = imag.astype(BF16)

    side_by_side([sum_angles, transform, store], group, wide)


def finish(base, partner, other, probe_mine, probe_theirs, psi_out, probe_out):
    mask = lane_mask(base.shape[1:], base.shape[-1] // 2)
    left, right = packed_sides(partner, other, is_even())
    real, imag = unfold(left, right, mask)
    psi_out[0, 0] = base[0] + real
    psi_out[1, 0] = base[1] + imag
    core = lax.axis_index("angle") % 2
    probe_out[core] = probe_mine[...]
    probe_out[1 - core] = probe_theirs[...]


VMEM = pl.BlockSpec(memory_space=pltpu.VMEM)
SMEM = pl.BlockSpec(memory_space=pltpu.SMEM)
HBM = pl.BlockSpec(memory_space=pltpu.HBM)
ANY = pl.BlockSpec(memory_space=pl.ANY)


def call(body, name, out_shape, in_specs, scratch=(), flops=0, size=0, **more):
    return pl.pallas_call(
        body,
        name=name,
        out_shape=out_shape,
        in_specs=in_specs,
        scratch_shapes=list(scratch),
        compiler_params=pltpu.CompilerParams(vmem_limit_bytes=VMEM_LIMIT),
        cost_estimate=pl.CostEstimate(flops=flops, bytes_accessed=size, transcendentals=0),
        **more,
    )


def shape(*dims, dtype=F32):
    return jax.ShapeDtypeStruct(dims, dtype)


def swap_pairs(array, start, tiles):
    low = range(start, tiles - 1, 2)
    return lax.ppermute(array, "tile", [(i, i + 1) for i in low] + [(i + 1, i) for i in low])


def exchange(to_partner, to_other, tiles):
    return swap_pairs(to_partner, 0, tiles), swap_pairs(to_other, 1, tiles)


def inner_count(tiles):
    return max(1, tiles // 4)


def swap(array, mask, devices):
    return lax.ppermute(array, ("angle", "tile"), [(i, i ^ mask) for i in range(devices)])


def hypercube(angles, tiles):
    bits = [tiles << at for at in range(1, angles.bit_length() - 1)]
    bits += [1 << at for at in range(tiles.bit_length() - 1)]
    rounds = []
    while bits:
        two, bits = bits[:2], bits[2:]
        rounds.append(two if len(two) == 1 else [two[0], two[1], two[0] ^ two[1]])
    return rounds


def shards(psi, target, probe, data, pos_z, pos_x, counts, shears):
    rows_total, width = psi.shape[2], psi.shape[3]
    side = probe.shape[1]
    angles, tiles = lax.axis_size("angle"), lax.axis_size("tile")
    devices = angles * tiles
    depth = rows_total // tiles
    beam = 32
    norm = 1.0 / math.sqrt(side)
    tables = [
        jnp.asarray(right_table(side, -1.0, norm)),
        jnp.asarray(left_table(side, -1.0, norm)),
        jnp.asarray(left_table(side, 1.0, norm)),
        jnp.asarray(right_table(side, 1.0, norm)),
    ]
    block = (2, rows_total, width)
    work = [
        pltpu.VMEM(block, F32),
        pltpu.VMEM(block, F32),
        pltpu.VMEM((2, side, side), F32),
        pltpu.VMEM((data.shape[2], 2, side, side), F32),
    ]
    slots = data.shape[2]
    flops = slots * 4 * 2 * side * 6 * side * 2 * side
    slot_places = [pltpu.with_memory_space_constraint(x, pltpu.HBM) for x in (pos_z, pos_x)]
    places = [pltpu.SMEM(x.shape, x.dtype) for x in slot_places] + [pltpu.SemaphoreType.DMA((2,))]
    psi = pltpu.with_memory_space_constraint(psi, pltpu.HBM)
    flat = shape(rows_total, width)
    to_partner, to_other = call(
        pack_kernel,
        "psi_pack",
        [flat] * 2,
        [HBM],
        [pltpu.VMEM(block, F32), pltpu.SemaphoreType.DMA((2,))],
    )(psi)
    partner, other = exchange(to_partner, to_other, tiles)
    operands = [
        pltpu.with_memory_space_constraint(x, pltpu.HBM)
        for x in [psi, target, probe, data] + tables
    ]
    psi_in, target_in, probe_in, data_in, *tables = call(
        stage_kernel,
        "stage_operands",
        [pltpu.VMEM(x.shape, x.dtype) for x in operands],
        [HBM] * len(operands),
        [pltpu.SemaphoreType.DMA((len(operands),))],
        0,
        3_000_000,
        out_specs=[VMEM] * len(operands),
    )(*operands)
    target_in, data_in, *tables = [
        pltpu.with_memory_space_constraint(x, pltpu.VMEM) for x in [target_in, data_in] + tables
    ]
    half = shape(side + 8, side)
    to_partner, to_other, base, rim, keep, send = call(
        first_kernel,
        "ptycho_first",
        [shape(*block)] * 4 + [half] * 2,
        [HBM] * 2 + [SMEM] * 2 + [VMEM] * 10,
        places + [pltpu.VMEM(block, F32)] + work,
        flops,
    )(*slot_places, counts, shears, psi_in, target_in, partner, other, probe_in, data_in, *tables)
    rounds = hypercube(angles, tiles)

    def all_but_last(keep, send, rounds):
        piece = shape(*keep.shape)
        total = call(sum_kernel, "probe_sum", piece, [VMEM] * 2)(keep, swap(send, tiles, devices))
        for masks in rounds[:-1]:
            terms = [total] + [swap(total, mask, devices) for mask in masks]
            total = call(sum_kernel, "probe_sum", piece, [VMEM] * len(terms))(*terms)
        return total

    def last_round(total, rounds):
        return [total] + [swap(total, mask, devices) for mask in rounds[-1]]

    terms = last_round(all_but_last(keep, send, rounds), rounds)
    partner, other = exchange(to_partner, to_other, tiles)
    probe_mine, extra = call(
        probe_kernel,
        "probe_step",
        [shape(side, side), shape(8, side)],
        [VMEM] * (1 + len(terms)),
        [pltpu.VMEM((side + 8, side), F32)],
    )(probe_in, *terms)
    probe_theirs = swap(probe_mine, tiles, devices)
    phases = call(
        functools.partial(phase_kernel, tiles),
        "phase_table",
        shape(angles, 3, tiles, beam, width),
        [VMEM],
        (),
        angles * tiles * beam * width * 40,
    )(extra)
    inner = inner_count(tiles)
    outer = tiles // inner
    base, to_partner, to_other, keep, send, *slabs = call(
        second_kernel,
        "ptycho_second",
        [shape(*block), flat, flat]
        + [shape(side, side)] * 2
        + [shape(outer, 4 * depth, width)] * inner,
        [HBM] * 2 + [SMEM] + [VMEM] * 12 + [ANY],
        places + [pltpu.VMEM(block, F32)] * 4 + [pltpu.VMEM((2, side, side), F32)] + work,
        flops,
    )(
        *(*slot_places, counts, base, rim, partner, other, target_in),
        *(probe_mine, probe_theirs, data_in, *tables, phases),
    )
    slabs = slabs[:1] + [swap(array, mask + 1, devices) for mask, array in enumerate(slabs[1:])]
    slabs = call(
        merge_kernel, "slab_merge", [shape(inner, 4 * depth, width)] * outer, [VMEM] * inner
    )(*slabs)
    slabs = [slabs[0]] + [swap(array, (mask + 1) * inner, devices) for mask, array in enumerate(slabs[1:])]
    total = all_but_last(keep, send, rounds)
    late, to_other = lax.optimization_barrier((total, to_other))
    other = swap_pairs(to_other, 1, tiles)
    for mask in rounds[-1][: 1 if len(rounds[-1]) > 1 else 0]:
        late = call(sum_kernel, "probe_sum", shape(*late.shape), [VMEM] * 2)(
            late, swap(late, mask, devices)
        )
    count = tiles * depth
    spectrum = call(
        forward_kernel,
        "slab_spectrum",
        shape(2 * count, width),
        [VMEM] * 2 + [ANY] + [VMEM] * outer,
        [pltpu.VMEM((count, 2 * width), F32), pltpu.VMEM((tiles, 4 * depth, width), F32)],
    )(
        jnp.asarray(twiddles(tiles, width, -1.0, 1.0)),
        jnp.asarray(right_table(width, -1.0, 1.0)),
        late,
        *slabs,
    )
    masks = list(range(angles))
    spectra = [spectrum] + [swap(spectrum, mask * tiles, devices) for mask in masks[1:]]
    late, spectra[1], to_partner = lax.optimization_barrier((late, spectra[1], to_partner))
    terms = [late, swap(late, rounds[-1][min(1, len(rounds[-1]) - 1)], devices)]
    partner = swap_pairs(to_partner, 0, tiles)
    probe_mine = call(
        last_probe_kernel,
        "probe_last",
        shape(side, side),
        [VMEM] * (2 + len(terms)),
        [pltpu.VMEM((side, side), F32)],
    )(probe_mine, extra, *terms)
    probe_theirs = swap(probe_mine, tiles, devices)
    scale = 1.0 / (angles * tiles * width)
    group = max(size for size in (1, 2, 4, 10) if depth % size == 0)
    last = (base, partner, other, probe_mine, probe_theirs)
    tomo, psi_new, probe_new = call(
        functools.partial(inverse_kernel, depth, masks),
        "slab_image",
        [
            shape(2, depth, beam, tiles * width, dtype=BF16),
            shape(2, 1, rows_total, width),
            shape(2, side, side),
        ],
        [VMEM] * (3 + angles + len(last)),
        [],
        depth * tiles * beam * 2 * 6 * width * 2 * width,
        grid=(depth // group,),
        out_specs=[
            pl.BlockSpec((2, group, beam, tiles * width), lambda row: (0, row, 0, 0)),
            pl.BlockSpec((2, 1, rows_total, width), lambda row: (0, 0, 0, 0)),
            pl.BlockSpec((2, side, side), lambda row: (0, 0, 0)),
        ],
    )(
        phases,
        jnp.asarray(twiddles(tiles, width, 1.0, scale)),
        jnp.asarray(right_table(width, 1.0, 1.0)),
        *spectra,
        *last,
    )
    return psi_new, probe_new, tomo


def solution(mesh):
    in_specs = (
        P(None, "angle", None, "tile"),
        P(None, "angle", None, "tile"),
        P(),
        P("angle", "tile", None, None, None),
        P("angle", "tile", None),
        P("angle", "tile", None),
        P("angle", "tile"),
        P("angle"),
    )
    out_specs = (P(None, "angle", None, "tile"), P(), P(None, "tile", "angle", None))
    return jax.shard_map(shards, mesh=mesh, in_specs=in_specs, out_specs=out_specs, check_vma=False)
```

```python
import functools
import math

import jax
import jax.numpy as jnp
import ml_dtypes
import numpy as np
from jax import lax
from jax.experimental import pallas as pl
from jax.experimental.pallas import tpu as pltpu
from jax.sharding import PartitionSpec as P

ITERS = 2
ALPHA = 0.004
RHO = 5.0
PROBE_STEP = 0.02
GROUP = 4
VMEM_LIMIT = 40 * 1024 * 1024
BF16 = jnp.bfloat16
F32 = jnp.float32


def split_table(matrix, axis):
    high = matrix.astype(ml_dtypes.bfloat16)
    low = (matrix - high.astype(np.float64)).astype(ml_dtypes.bfloat16)
    return np.concatenate([high, high, low], axis)


def dft_parts(length, orient, scale):
    counter = np.arange(length)
    angle = 2.0 * math.pi / length * (np.outer(counter, counter) % length)
    return np.cos(angle) * scale, orient * np.sin(angle) * scale


def right_table(length, orient, scale):
    real, imag = dft_parts(length, orient, scale)
    return split_table(np.block([[real, imag], [-imag, real]]), 0)


def left_table(length, orient, scale):
    real, imag = dft_parts(length, orient, scale)
    matrix = np.block([[real, -imag], [imag, real]])
    high = matrix.astype(ml_dtypes.bfloat16)
    return np.concatenate([high, (matrix - high.astype(np.float64)).astype(ml_dtypes.bfloat16)], 0)


def twiddles(tiles, inner, orient, scale):
    angle = 2.0 * math.pi / (tiles * inner) * np.outer(np.arange(tiles), np.arange(inner))
    return np.stack([np.cos(angle) * scale, orient * np.sin(angle) * scale]).astype(np.float32)


def halves(value):
    high = value.astype(BF16)
    low = (value - high.astype(F32)).astype(BF16)
    return high, low


def dot(left, right):
    return jnp.dot(left, right, preferred_element_type=F32)


def tall(table, high, low):
    size = high.shape[0]
    both = dot(table[...], high)
    return both[:size] + both[size:] + dot(table[0:size], low)


def butterfly(parts, orient):
    count = len(parts)
    if count == 1:
        return parts
    even = butterfly(parts[0::2], orient)
    odd = butterfly(parts[1::2], orient)
    low, high = [], []
    for index in range(count // 2):
        angle = orient * 2.0 * math.pi * index / count
        real, imag = odd[index]
        if index == 0:
            turned = (real, imag)
        elif 4 * index == count:
            turned = (-imag, real) if orient > 0 else (imag, -real)
        elif 8 * index in (count, 3 * count):
            tangent = orient if 8 * index == count else -orient
            plus, minus = (real + imag, imag - real)
            turned = (-minus, plus) if tangent > 0 else (plus, minus)
            turned = tuple(math.cos(angle) * value for value in turned)
        else:
            cosine, sine = math.cos(angle), math.sin(angle)
            turned = (real * cosine - imag * sine, real * sine + imag * cosine)
        base_real, base_imag = even[index]
        low.append((base_real + turned[0], base_imag + turned[1]))
        high.append((base_real - turned[0], base_imag - turned[1]))
    return low + high


def lane_mask(shape, half):
    return lax.broadcasted_iota(jnp.int32, shape, len(shape) - 1) < half


def side_by_side(stages, count, group):
    groups = count // group
    held = [None] * groups
    for turn in range(groups + len(stages) - 1):
        for number in reversed(range(len(stages))):
            at = turn - number
            if 0 <= at < groups:
                held[at] = stages[number](at * group, held[at])


def slot_loop(pos_z, pos_x, count, probe_real, probe_imag, data, tables, own, halo, work):
    right_fwd, left_fwd, left_inv, right_inv = tables
    grad_own, grad_halo, grad_probe, patches = work
    side = data.shape[-1]
    half = side // 2
    slots = data.shape[2]
    group = math.gcd(slots, GROUP)
    wide = math.gcd(group, 2)
    lanes = lax.broadcasted_iota(jnp.int32, (8, side), 1)
    grad_own[...] = jnp.zeros_like(grad_own)
    grad_halo[...] = jnp.zeros_like(grad_halo)
    grad_probe[...] = jnp.zeros_like(grad_probe)

    def place(slot):
        start = pos_x[0, 0, slot] - half
        back = jnp.where(start > 0, side - start, -start)
        forth = jnp.where(start < 0, side + start, start)
        inside = (lanes >= start) & (lanes < side + start)
        return pl.ds(pos_z[0, 0, slot], side), back, forth, inside

    def pick(inside, yes, no):
        rows = (side // 8, 8, side)
        return jnp.where(inside[None], yes.reshape(rows), no.reshape(rows)).reshape(side, side)

    def cut_out(first, _):
        waves = []
        for slot in range(first, first + group):
            where, back, _, inside = place(slot)
            cut = []
            for part in range(2):
                mixed = pick(inside, own[part, where, :], halo[part, where, :])
                cut.append(pltpu.roll(mixed, back, 1))
                patches[slot, part] = cut[part]
            waves.append(
                jnp.concatenate(
                    [
                        probe_real[...] * cut[0] - probe_imag[...] * cut[1],
                        probe_real[...] * cut[1] + probe_imag[...] * cut[0],
                    ],
                    1,
                )
            )
        return halves(jnp.concatenate(waves, 0))

    def rows_forward(first, split):
        high, low = split
        rows = dot(jnp.concatenate([high, low, high], 1), right_fwd[...])
        stacks = []
        for at in range(0, group, wide):
            some = [rows[(at + k) * side : (at + k + 1) * side] for k in range(wide)]
            stacked = jnp.concatenate(
                [
                    jnp.concatenate([block[:, :side] for block in some], 1),
                    jnp.concatenate([block[:, side:] for block in some], 1),
                ],
                0,
            )
            stacks.append(halves(stacked))
        return stacks

    def columns_forward(first, stacks):
        results = []
        for index, (high, low) in enumerate(stacks):
            far = tall(left_fwd, high, low)
            weights = []
            for k in range(wide):
                slot = first + index * wide + k
                live = jnp.where(slot < count, 1.0, 0.0).astype(F32)
                far_real = far[:side, k * side : (k + 1) * side]
                far_imag = far[side:, k * side : (k + 1) * side]
                weights.append((far_real * far_real + far_imag * far_imag - data[0, 0, slot]) * live)
            weight = jnp.concatenate(weights, 1)
            results.append(halves(jnp.concatenate([far[:side] * weight, far[side:] * weight], 0)))
        return results

    def columns_inverse(first, stacks):
        blocks = []
        for high, low in stacks:
            back_cols = tall(left_inv, high, low)
            for k in range(wide):
                block = back_cols[:, k * side : (k + 1) * side]
                blocks.append(jnp.concatenate([block[:side], block[side:]], 1))
        return halves(jnp.concatenate(blocks, 0))

    def rows_inverse(first, split):
        high, low = split
        return dot(jnp.concatenate([high, low, high], 1), right_inv[...])

    def add_back(first, chi):
        sum_real, sum_imag = grad_probe[0], grad_probe[1]
        for member in range(group):
            slot = first + member
            where, _, forth, inside = place(slot)
            chi_real = chi[member * side : (member + 1) * side, :side]
            chi_imag = chi[member * side : (member + 1) * side, side:]
            cut_real, cut_imag = patches[slot, 0], patches[slot, 1]
            sum_real = sum_real + (cut_real * chi_real + cut_imag * chi_imag)
            sum_imag = sum_imag + (cut_real * chi_imag - cut_imag * chi_real)
            grads = (
                probe_real[...] * chi_real + probe_imag[...] * chi_imag,
                probe_real[...] * chi_imag - probe_imag[...] * chi_real,
            )
            for part in range(2):
                moved = pltpu.roll(grads[part], forth, 1)
                zero = jnp.zeros_like(moved)
                grad_own[part, where, :] += pick(inside, moved, zero)
                grad_halo[part, where, :] += pick(inside, zero, moved)
        grad_probe[0], grad_probe[1] = sum_real, sum_imag

    side_by_side(
        [cut_out, rows_forward, columns_forward, columns_inverse, rows_inverse, add_back], slots, group
    )


def stage_kernel(*refs):
    count = (len(refs) - 1) // 2
    copies = [
        pltpu.make_async_copy(refs[index], refs[count + index], refs[-1].at[index])
        for index in range(count)
    ]
    for copy in copies:
        copy.start()
    for copy in copies:
        copy.wait()


def sides(partner, other, part, even):
    first, second = partner[part], other[part]
    return jnp.where(even, second, first), jnp.where(even, first, second)


def is_even():
    return lax.axis_index("tile") % 2 == 0


def load_places(sources, targets, sems):
    copies = [
        pltpu.make_async_copy(source, target, sems.at[index])
        for index, (source, target) in enumerate(zip(sources, targets))
    ]
    for copy in copies:
        copy.start()
    return copies


def fold(kept, turned, mask):
    return jnp.where(mask, kept, pltpu.roll(turned, mask.shape[-1] // 2, 1))


def pack_kernel(psi, to_partner, to_other, held, sems):
    copies = [pltpu.make_async_copy(psi.at[part, 0], held.at[part], sems.at[part]) for part in range(2)]
    for copy in copies:
        copy.start()
    mask = lane_mask(to_partner.shape, to_partner.shape[-1] // 2)
    even = is_even()
    for copy in copies:
        copy.wait()
    to_left = fold(held[0], held[1], mask)
    to_right = fold(held[0], held[1], ~mask)
    to_partner[...] = jnp.where(even, to_right, to_left)
    to_other[...] = jnp.where(even, to_left, to_right)


def unfold(low_source, high_source, mask):
    real = jnp.where(mask, low_source, high_source)
    imag = pltpu.roll(jnp.where(mask, high_source, low_source), mask.shape[-1] // 2, 1)
    return real, imag


def packed_sides(partner, other, even):
    first, second = partner[...], other[...]
    return jnp.where(even, second, first), jnp.where(even, first, second)


def first_kernel(
    pos_z, pos_x, counts, shears, psi, target, partner, other, probe, data, *rest
):
    tables = rest[:4]
    to_partner, to_other, base_out, rim_out, keep_out, send_out = rest[4:10]
    held, sems, halo, work = rest[10:12], rest[12], rest[13], rest[14:]
    copies = load_places((pos_z, pos_x), held, sems)
    pos_z, pos_x = held
    grad_own, grad_halo, grad_probe = work[:3]
    side = data.shape[-1]
    mask = lane_mask(psi.shape[2:], side // 2)
    even = is_even()
    left, right = packed_sides(partner, other, even)
    halo[0], halo[1] = unfold(right, left, mask)
    for copy in copies:
        copy.wait()
    count = counts[0, 0]
    slot_loop(
        pos_z, pos_x, count, probe.at[0], probe.at[1], data, tables, psi.at[:, 0], halo, work
    )
    for part in range(2):
        field = psi[part, 0]
        base = field - ALPHA * (grad_own[part] + RHO * (field - target[part, 0]))
        rim = -ALPHA * grad_halo[part]
        base_out[part] = base
        rim_out[part] = rim
        to_right, to_left = jnp.where(mask, rim, base), jnp.where(mask, base, rim)
        to_partner[part] = jnp.where(even, to_right, to_left)
        to_other[part] = jnp.where(even, to_left, to_right)
    row = lax.broadcasted_iota(jnp.int32, (8, side), 0)
    lane = lax.broadcasted_iota(jnp.int32, (8, side), 1)
    angle, tile = lax.axis_index("angle"), lax.axis_index("tile")
    mine = (row == 1) & (lane == angle) & (tile % inner_count(lax.axis_size("tile")) == 0)
    extra = jnp.where(row == 0, count.astype(F32), jnp.where(mine, shears[0], 0.0))
    core = angle % 2
    for out, part in ((keep_out, core), (send_out, 1 - core)):
        out[0:side] = grad_probe[part]
        out[side : side + 8] = extra


def sum_kernel(*refs):
    terms = [ref[...] for ref in refs[:-1]]
    while len(terms) > 1:
        terms = [terms[at] + terms[at + 1] for at in range(0, len(terms), 2)]
    refs[-1][...] = terms[0]


def probe_kernel(_, probe, *refs):
    total, probe_out, extra_out = refs[-1], refs[-3], refs[-2]
    sum_kernel(*refs[:-3], total)
    side = probe.shape[-1]
    extra = total[side : side + 8]
    part = lax.axis_index("angle") % 2
    probe_out[...] = probe[part] - PROBE_STEP * total[0:side] / extra[0:1]
    extra_out[...] = extra


def last_probe_kernel(probe_mine, extra, *refs):
    total, probe_out = refs[-1], refs[-2]
    sum_kernel(*refs[:-2], total)
    probe_out[...] = probe_mine[...] - PROBE_STEP * total[...] / extra[0:1]


def second_kernel(
    pos_z, pos_x, counts, base, rim, partner, other, target, probe_mine, probe_theirs, data, *rest
):
    tables = rest[:4]
    base_out, to_partner, to_other, keep_out, send_out = rest[5:10]
    inner = inner_count(lax.axis_size("tile"))
    slab_outs, rest = rest[10 : 10 + inner], rest[10 + inner :]
    held, sems, own, halo, hold, edge, probe, work = rest[:2], *rest[2:8], rest[8:]
    copies = load_places((pos_z, pos_x), held, sems)
    pos_z, pos_x = held
    grad_own, grad_halo, grad_probe = work[:3]
    side = data.shape[-1]
    mask = lane_mask(base.shape[1:], side // 2)
    tile, tiles = lax.axis_index("tile"), lax.axis_size("tile")
    from_right = jnp.where(tile < tiles - 1, 1.0, 0.0).astype(F32)
    from_left = jnp.where(tile > 0, 1.0, 0.0).astype(F32)
    core = lax.axis_index("angle") % 2
    probe[core] = probe_mine[...]
    probe[1 - core] = probe_theirs[...]
    even = is_even()
    for part in range(2):
        left, right = sides(partner, other, part, even)
        own[part] = base[part] + jnp.where(mask, left, right)
        halo[part] = jnp.where(
            mask, (right + rim[part]) * from_right, (left + rim[part]) * from_left
        )
    for copy in copies:
        copy.wait()
    slot_loop(
        pos_z, pos_x, counts[0, 0], probe.at[0], probe.at[1], data, tables, own, halo, work
    )
    for part in range(2):
        field = own[part]
        aim = target[part, 0]
        updated = field - ALPHA * (grad_own[part] + RHO * (field - aim))
        edge[part] = -ALPHA * grad_halo[part]
        base_out[part] = updated
        hold[part] = aim - updated
    to_right = fold(edge[0], edge[1], mask)
    to_left = fold(edge[0], edge[1], ~mask)
    to_partner[...] = jnp.where(even, to_right, to_left)
    to_other[...] = jnp.where(even, to_left, to_right)
    keep_out[...] = grad_probe[core]
    send_out[...] = grad_probe[1 - core]
    outer, depth = slab_outs[0].shape[0], slab_outs[0].shape[1] // 4
    for step, slab_out in enumerate(slab_outs):
        for place in range(outer):
            slab = place * inner + ((tile % inner) ^ step)
            rows = pl.ds(slab * depth, depth)
            for part in range(2):
                slab_out[place, part * depth : (part + 1) * depth] = hold[part, rows]
                slab_out[place, (2 + part) * depth : (3 + part) * depth] = edge[part, rows]


def merge_kernel(*refs):
    tile = lax.axis_index("tile")
    inner = inner_count(lax.axis_size("tile"))
    arrived, merged = refs[:inner], refs[inner:]
    for step, source in enumerate(arrived):
        for mask, out in enumerate(merged):
            out[(tile % inner) ^ step] = source[(tile // inner) ^ mask]


def forward_kernel(turn, table, _, *rest):
    *arrived, spectrum_out, rows_scratch, slabs = rest
    inner, _, width = arrived[0].shape
    tiles = slabs.shape[0]
    depth = rows_scratch.shape[0] // tiles
    outer = lax.axis_index("tile") // inner
    for mask, source in enumerate(arrived):
        slabs[pl.ds((outer ^ mask) * inner, inner)] = source[...]
    mask = lane_mask((depth, width), width // 2)
    blocks = []
    for tile in range(tiles):
        block = []
        for part in range(2):
            rows = slice((2 + part) * depth, (3 + part) * depth)
            zero = jnp.zeros((depth, width), F32)
            before = slabs[tile - 1, rows] if tile > 0 else zero
            after = slabs[tile + 1, rows] if tile < tiles - 1 else zero
            block.append(
                slabs[tile, part * depth : (part + 1) * depth] - jnp.where(mask, before, after)
            )
        blocks.append(tuple(block))
    for index, (real, imag) in enumerate(butterfly(blocks, -1)):
        cosine, sine = turn[0, index : index + 1], turn[1, index : index + 1]
        rows = slice(index * depth, (index + 1) * depth)
        rows_scratch[rows, :width] = real * cosine - imag * sine
        rows_scratch[rows, width:] = real * sine + imag * cosine
    high, low = halves(rows_scratch[...])
    spectrum = dot(jnp.concatenate([high, low, high], 1), table[...])
    count = rows_scratch.shape[0]
    spectrum_out[0:count] = spectrum[:, :width]
    spectrum_out[count : 2 * count] = spectrum[:, width:]


def phase_kernel(tiles, sums, table_out):
    angles, _, _, beam, width = table_out.shape
    total = tiles * width
    first = lax.axis_index("angle") * beam - (beam * lax.axis_size("angle")) // 2
    offsets = (lax.broadcasted_iota(jnp.int32, (beam, width), 0) + first).astype(F32)
    column = lax.broadcasted_iota(jnp.int32, (beam, width), 1)
    for angle in range(angles):
        shear = sums[sums.shape[0] - 7 : sums.shape[0] - 6, angle : angle + 1]
        for block in range(tiles):
            frequency = block + tiles * column
            signed = jnp.where(frequency < total // 2, frequency, frequency - total).astype(F32)
            turns = (offsets * signed * shear) * (1.0 / total)
            turns = turns - jnp.floor(turns + 0.5)
            x = turns * math.pi
            square = x * x
            sine = x * (
                1.0 + square * (-1 / 6 + square * (1 / 120 + square * (-1 / 5040 + square * (
                    1 / 362880 + square * (-1 / 39916800 + square * (1.0 / 6227020800.0))))))
            )
            cosine = 1.0 + square * (-1 / 2 + square * (1 / 24 + square * (-1 / 720 + square * (
                1 / 40320 + square * (-1 / 3628800 + square * (1.0 / 479001600.0))))))
            real = 1.0 - 2.0 * sine * sine
            imag = 2.0 * sine * cosine
            table_out[angle, 0, block] = real
            table_out[angle, 1, block] = imag - real
            table_out[angle, 2, block] = real + imag


def inverse_kernel(depth, masks, phases, turn, table, *rest):
    spectra = rest[: len(masks)]
    last, outs = rest[len(masks) : -7], rest[-7:-4]
    (image, psi, probe), sems = rest[-4:-1], rest[-1]
    _, _, tiles, beam, width = phases.shape
    angles = [lax.axis_index("angle") ^ mask for mask in masks]
    finish(*last, psi, probe)
    copies = [
        pltpu.make_async_copy(psi, outs[1], sems.at[0]),
        pltpu.make_async_copy(probe, outs[2], sems.at[1]),
    ]
    for copy in copies:
        copy.start()
    wide = math.gcd(depth, 2)
    count = tiles * depth

    def sum_angles(start, _):
        rows = [[] for _ in range(wide)]
        for block in range(tiles):
            tables = [[phases[angle, which, block] for which in range(3)] for angle in angles]
            for member in range(wide):
                at = block * depth + start + member
                sums = None
                for spectrum, three in zip(spectra, tables):
                    real = spectrum[pl.ds(at, 1), :]
                    imag = spectrum[pl.ds(count + at, 1), :]
                    terms = [factor * one for factor, one in zip((real + imag, real, imag), three)]
                    sums = terms if sums is None else [x + y for x, y in zip(sums, terms)]
                rows[member].append(jnp.concatenate([sums[0] - sums[2], sums[0] + sums[1]], 1))
        return [halves(jnp.concatenate(blocks, 0)) for blocks in rows]

    def transform(start, splits):
        return [dot(jnp.concatenate([high, low, high], 1), table[...]) for high, low in splits]

    def store(start, images):
        for member, one in enumerate(images):
            blocks = []
            for block in range(tiles):
                real = one[block * beam : (block + 1) * beam, :width]
                imag = one[block * beam : (block + 1) * beam, width:]
                cosine, sine = turn[0, block : block + 1], turn[1, block : block + 1]
                blocks.append((real * cosine - imag * sine, real * sine + imag * cosine))
            for index, (real, imag) in enumerate(butterfly(blocks, 1)):
                columns = slice(index * width, (index + 1) * width)
                image[0, start + member, :, columns] = real.astype(BF16)
                image[1, start + member, :, columns] = imag.astype(BF16)
        rows = pl.ds(start, wide)
        copy = pltpu.make_async_copy(image.at[:, rows], outs[0].at[:, rows], sems.at[2 + start // wide])
        copy.start()
        copies.append(copy)

    side_by_side([sum_angles, transform, store], depth, wide)
    for copy in copies:
        copy.wait()


def finish(base, partner, other, probe_mine, probe_theirs, psi_out, probe_out):
    mask = lane_mask(base.shape[1:], base.shape[-1] // 2)
    left, right = packed_sides(partner, other, is_even())
    real, imag = unfold(left, right, mask)
    psi_out[0, 0] = base[0] + real
    psi_out[1, 0] = base[1] + imag
    core = lax.axis_index("angle") % 2
    probe_out[core] = probe_mine[...]
    probe_out[1 - core] = probe_theirs[...]


VMEM = pl.BlockSpec(memory_space=pltpu.VMEM)
SMEM = pl.BlockSpec(memory_space=pltpu.SMEM)
HBM = pl.BlockSpec(memory_space=pltpu.HBM)
ANY = pl.BlockSpec(memory_space=pl.ANY)


def call(body, name, out_shape, in_specs, scratch=(), flops=0, size=0, **more):
    return pl.pallas_call(
        body,
        name=name,
        out_shape=out_shape,
        in_specs=in_specs,
        scratch_shapes=list(scratch),
        compiler_params=pltpu.CompilerParams(vmem_limit_bytes=VMEM_LIMIT),
        cost_estimate=pl.CostEstimate(flops=flops, bytes_accessed=size, transcendentals=0),
        **more,
    )


def shape(*dims, dtype=F32):
    return jax.ShapeDtypeStruct(dims, dtype)


def swap_pairs(array, start, tiles):
    low = range(start, tiles - 1, 2)
    return lax.ppermute(array, "tile", [(i, i + 1) for i in low] + [(i + 1, i) for i in low])


def exchange(to_partner, to_other, tiles):
    return swap_pairs(to_partner, 0, tiles), swap_pairs(to_other, 1, tiles)


def inner_count(tiles):
    return max(1, tiles // 4)


def swap(array, mask, devices):
    return lax.ppermute(array, ("angle", "tile"), [(i, i ^ mask) for i in range(devices)])


def hypercube(angles, tiles):
    bits = [tiles << at for at in range(1, angles.bit_length() - 1)]
    bits += [1 << at for at in range(tiles.bit_length() - 1)]
    rounds = []
    while bits:
        two, bits = bits[:2], bits[2:]
        rounds.append(two if len(two) == 1 else [two[0], two[1], two[0] ^ two[1]])
    return rounds


def shards(psi, target, probe, data, pos_z, pos_x, counts, shears):
    rows_total, width = psi.shape[2], psi.shape[3]
    side = probe.shape[1]
    angles, tiles = lax.axis_size("angle"), lax.axis_size("tile")
    devices = angles * tiles
    depth = rows_total // tiles
    beam = 32
    norm = 1.0 / math.sqrt(side)
    tables = [
        jnp.asarray(right_table(side, -1.0, norm)),
        jnp.asarray(left_table(side, -1.0, norm)),
        jnp.asarray(left_table(side, 1.0, norm)),
        jnp.asarray(right_table(side, 1.0, norm)),
    ]
    block = (2, rows_total, width)
    work = [
        pltpu.VMEM(block, F32),
        pltpu.VMEM(block, F32),
        pltpu.VMEM((2, side, side), F32),
        pltpu.VMEM((data.shape[2], 2, side, side), F32),
    ]
    slots = data.shape[2]
    flops = slots * 4 * 2 * side * 6 * side * 2 * side
    slot_places = [pltpu.with_memory_space_constraint(x, pltpu.HBM) for x in (pos_z, pos_x)]
    places = [pltpu.SMEM(x.shape, x.dtype) for x in slot_places] + [pltpu.SemaphoreType.DMA((2,))]
    psi = pltpu.with_memory_space_constraint(psi, pltpu.HBM)
    flat = shape(rows_total, width)
    to_partner, to_other = call(
        pack_kernel,
        "psi_pack",
        [flat] * 2,
        [HBM],
        [pltpu.VMEM(block, F32), pltpu.SemaphoreType.DMA((2,))],
    )(psi)
    partner, other = exchange(to_partner, to_other, tiles)
    operands = [
        pltpu.with_memory_space_constraint(x, pltpu.HBM)
        for x in [psi, target, probe, data] + tables
    ]
    psi_in, target_in, probe_in, data_in, *tables = call(
        stage_kernel,
        "stage_operands",
        [pltpu.VMEM(x.shape, x.dtype) for x in operands],
        [HBM] * len(operands),
        [pltpu.SemaphoreType.DMA((len(operands),))],
        0,
        3_000_000,
        out_specs=[VMEM] * len(operands),
    )(*operands)
    target_in, data_in, *tables = [
        pltpu.with_memory_space_constraint(x, pltpu.VMEM) for x in [target_in, data_in] + tables
    ]
    half = shape(side + 8, side)
    to_partner, to_other, base, rim, keep, send = call(
        first_kernel,
        "ptycho_first",
        [shape(*block)] * 4 + [half] * 2,
        [HBM] * 2 + [SMEM] * 2 + [VMEM] * 10,
        places + [pltpu.VMEM(block, F32)] + work,
        flops,
    )(*slot_places, counts, shears, psi_in, target_in, partner, other, probe_in, data_in, *tables)
    rounds = hypercube(angles, tiles)

    def all_but_last(keep, send, rounds):
        piece = shape(*keep.shape)
        total = call(sum_kernel, "probe_sum", piece, [VMEM] * 2)(keep, swap(send, tiles, devices))
        for masks in rounds[:-1]:
            terms = [total] + [swap(total, mask, devices) for mask in masks]
            total = call(sum_kernel, "probe_sum", piece, [VMEM] * len(terms))(*terms)
        return total

    def last_round(total, rounds):
        return [total] + [swap(total, mask, devices) for mask in rounds[-1]]

    nearly = all_but_last(keep, send, rounds)
    terms = last_round(nearly, rounds)
    partner, other = exchange(to_partner, to_other, tiles)
    phases = call(
        functools.partial(phase_kernel, tiles),
        "phase_table",
        shape(angles, 3, tiles, beam, width),
        [VMEM],
        (),
        angles * tiles * beam * width * 40,
    )(nearly)
    probe_mine, extra = call(
        probe_kernel,
        "probe_step",
        [shape(side, side), shape(8, side)],
        [ANY] + [VMEM] * (1 + len(terms)),
        [pltpu.VMEM((side + 8, side), F32)],
    )(phases, probe_in, *terms)
    probe_theirs = swap(probe_mine, tiles, devices)
    inner = inner_count(tiles)
    outer = tiles // inner
    base, to_partner, to_other, keep, send, *slabs = call(
        second_kernel,
        "ptycho_second",
        [shape(*block), flat, flat]
        + [shape(side, side)] * 2
        + [shape(outer, 4 * depth, width)] * inner,
        [HBM] * 2 + [SMEM] + [VMEM] * 12 + [ANY],
        places + [pltpu.VMEM(block, F32)] * 4 + [pltpu.VMEM((2, side, side), F32)] + work,
        flops,
    )(
        *(*slot_places, counts, base, rim, partner, other, target_in),
        *(probe_mine, probe_theirs, data_in, *tables, phases),
    )
    slabs = slabs[:1] + [swap(array, mask + 1, devices) for mask, array in enumerate(slabs[1:])]
    slabs = call(
        merge_kernel, "slab_merge", [shape(inner, 4 * depth, width)] * outer, [VMEM] * inner
    )(*slabs)
    slabs = [slabs[0]] + [swap(array, (mask + 1) * inner, devices) for mask, array in enumerate(slabs[1:])]
    total = all_but_last(keep, send, rounds)
    late, to_other = lax.optimization_barrier((total, to_other))
    other = swap_pairs(to_other, 1, tiles)
    for mask in rounds[-1][: 1 if len(rounds[-1]) > 1 else 0]:
        late = call(sum_kernel, "probe_sum", shape(*late.shape), [VMEM] * 2)(
            late, swap(late, mask, devices)
        )
    count = tiles * depth
    spectrum = call(
        forward_kernel,
        "slab_spectrum",
        shape(2 * count, width),
        [VMEM] * 2 + [ANY] + [VMEM] * outer,
        [pltpu.VMEM((count, 2 * width), F32), pltpu.VMEM((tiles, 4 * depth, width), F32)],
    )(
        jnp.asarray(twiddles(tiles, width, -1.0, 1.0)),
        jnp.asarray(right_table(width, -1.0, 1.0)),
        late,
        *slabs,
    )
    masks = list(range(angles))
    spectra = [spectrum] + [swap(spectrum, mask * tiles, devices) for mask in masks[1:]]
    late, spectra[1], to_partner = lax.optimization_barrier((late, spectra[1], to_partner))
    terms = [late, swap(late, rounds[-1][min(1, len(rounds[-1]) - 1)], devices)]
    partner = swap_pairs(to_partner, 0, tiles)
    probe_mine = call(
        last_probe_kernel,
        "probe_last",
        shape(side, side),
        [VMEM] * (2 + len(terms)),
        [pltpu.VMEM((side, side), F32)],
    )(probe_mine, extra, *terms)
    probe_theirs = swap(probe_mine, tiles, devices)
    scale = 1.0 / (angles * tiles * width)
    last = (base, partner, other, probe_mine, probe_theirs)
    tomo, psi_new, probe_new = call(
        functools.partial(inverse_kernel, depth, masks),
        "slab_image",
        [
            shape(2, depth, beam, tiles * width, dtype=BF16),
            shape(2, 1, rows_total, width),
            shape(2, side, side),
        ],
        [VMEM] * (3 + angles + len(last)),
        [
            pltpu.VMEM((2, depth, beam, tiles * width), BF16),
            pltpu.VMEM((2, 1, rows_total, width), F32),
            pltpu.VMEM((2, side, side), F32),
            pltpu.SemaphoreType.DMA((2 + depth // math.gcd(depth, 2),)),
        ],
        depth * tiles * beam * 2 * 6 * width * 2 * width,
        out_specs=[HBM] * 3,
    )(
        phases,
        jnp.asarray(twiddles(tiles, width, 1.0, scale)),
        jnp.asarray(right_table(width, 1.0, 1.0)),
        *spectra,
        *last,
    )
    return psi_new, probe_new, tomo


def solution(mesh):
    in_specs = (
        P(None, "angle", None, "tile"),
        P(None, "angle", None, "tile"),
        P(),
        P("angle", "tile", None, None, None),
        P("angle", "tile", None),
        P("angle", "tile", None),
        P("angle", "tile"),
        P("angle"),
    )
    out_specs = (P(None, "angle", None, "tile"), P(), P(None, "tile", "angle", None))
    return jax.shard_map(shards, mesh=mesh, in_specs=in_specs, out_specs=out_specs, check_vma=False)
```

```python
import functools
import math

import jax
import jax.numpy as jnp
import ml_dtypes
import numpy as np
from jax import lax
from jax.experimental import pallas as pl
from jax.experimental.pallas import tpu as pltpu
from jax.sharding import PartitionSpec as P

ITERS = 2
ALPHA = 0.004
RHO = 5.0
PROBE_STEP = 0.02
GROUP = 4
VMEM_LIMIT = 40 * 1024 * 1024
BF16 = jnp.bfloat16
F32 = jnp.float32


def split_table(matrix, axis):
    high = matrix.astype(ml_dtypes.bfloat16)
    low = (matrix - high.astype(np.float64)).astype(ml_dtypes.bfloat16)
    return np.concatenate([high, high, low], axis)


def dft_parts(length, orient, scale):
    counter = np.arange(length)
    angle = 2.0 * math.pi / length * (np.outer(counter, counter) % length)
    return np.cos(angle) * scale, orient * np.sin(angle) * scale


def right_table(length, orient, scale):
    real, imag = dft_parts(length, orient, scale)
    return split_table(np.block([[real, imag], [-imag, real]]), 0)


def left_table(length, orient, scale):
    real, imag = dft_parts(length, orient, scale)
    matrix = np.block([[real, -imag], [imag, real]])
    high = matrix.astype(ml_dtypes.bfloat16)
    return np.concatenate([high, (matrix - high.astype(np.float64)).astype(ml_dtypes.bfloat16)], 0)


def twiddles(tiles, inner, orient, scale):
    angle = 2.0 * math.pi / (tiles * inner) * np.outer(np.arange(tiles), np.arange(inner))
    return np.stack([np.cos(angle) * scale, orient * np.sin(angle) * scale]).astype(np.float32)


def halves(value):
    high = value.astype(BF16)
    low = (value - high.astype(F32)).astype(BF16)
    return high, low


def dot(left, right):
    return jnp.dot(left, right, preferred_element_type=F32)


def tall(table, high, low):
    size = high.shape[0]
    both = dot(table[...], high)
    return both[:size] + both[size:] + dot(table[0:size], low)


def butterfly(parts, orient):
    count = len(parts)
    if count == 1:
        return parts
    even = butterfly(parts[0::2], orient)
    odd = butterfly(parts[1::2], orient)
    low, high = [], []
    for index in range(count // 2):
        angle = orient * 2.0 * math.pi * index / count
        real, imag = odd[index]
        if index == 0:
            turned = (real, imag)
        elif 4 * index == count:
            turned = (-imag, real) if orient > 0 else (imag, -real)
        elif 8 * index in (count, 3 * count):
            tangent = orient if 8 * index == count else -orient
            plus, minus = (real + imag, imag - real)
            turned = (-minus, plus) if tangent > 0 else (plus, minus)
            turned = tuple(math.cos(angle) * value for value in turned)
        else:
            cosine, sine = math.cos(angle), math.sin(angle)
            turned = (real * cosine - imag * sine, real * sine + imag * cosine)
        base_real, base_imag = even[index]
        low.append((base_real + turned[0], base_imag + turned[1]))
        high.append((base_real - turned[0], base_imag - turned[1]))
    return low + high


def lane_mask(shape, half):
    return lax.broadcasted_iota(jnp.int32, shape, len(shape) - 1) < half


def side_by_side(stages, count, group):
    groups = count // group
    held = [None] * groups
    for turn in range(groups + len(stages) - 1):
        for number in reversed(range(len(stages))):
            at = turn - number
            if 0 <= at < groups:
                held[at] = stages[number](at * group, held[at])


def slot_loop(pos_z, pos_x, count, probe_real, probe_imag, data, tables, own, halo, work):
    right_fwd, left_fwd, left_inv, right_inv = tables
    grad_own, grad_halo, grad_probe, patches = work
    side = data.shape[-1]
    half = side // 2
    slots = data.shape[2]
    group = math.gcd(slots, GROUP)
    wide = math.gcd(group, 2)
    lanes = lax.broadcasted_iota(jnp.int32, (8, side), 1)
    grad_own[...] = jnp.zeros_like(grad_own)
    grad_halo[...] = jnp.zeros_like(grad_halo)
    grad_probe[...] = jnp.zeros_like(grad_probe)

    def place(slot):
        start = pos_x[0, 0, slot] - half
        back = jnp.where(start > 0, side - start, -start)
        forth = jnp.where(start < 0, side + start, start)
        inside = (lanes >= start) & (lanes < side + start)
        return pl.ds(pos_z[0, 0, slot], side), back, forth, inside

    def pick(inside, yes, no):
        rows = (side // 8, 8, side)
        return jnp.where(inside[None], yes.reshape(rows), no.reshape(rows)).reshape(side, side)

    def cut_out(first, _):
        waves = []
        for slot in range(first, first + group):
            where, back, _, inside = place(slot)
            cut = []
            for part in range(2):
                mixed = pick(inside, own[part, where, :], halo[part, where, :])
                cut.append(pltpu.roll(mixed, back, 1))
                patches[slot, part] = cut[part]
            waves.append(
                jnp.concatenate(
                    [
                        probe_real[...] * cut[0] - probe_imag[...] * cut[1],
                        probe_real[...] * cut[1] + probe_imag[...] * cut[0],
                    ],
                    1,
                )
            )
        return halves(jnp.concatenate(waves, 0))

    def rows_forward(first, split):
        high, low = split
        rows = dot(jnp.concatenate([high, low, high], 1), right_fwd[...])
        stacks = []
        for at in range(0, group, wide):
            some = [rows[(at + k) * side : (at + k + 1) * side] for k in range(wide)]
            stacked = jnp.concatenate(
                [
                    jnp.concatenate([block[:, :side] for block in some], 1),
                    jnp.concatenate([block[:, side:] for block in some], 1),
                ],
                0,
            )
            stacks.append(halves(stacked))
        return stacks

    def columns_forward(first, stacks):
        results = []
        for index, (high, low) in enumerate(stacks):
            far = tall(left_fwd, high, low)
            weights = []
            for k in range(wide):
                slot = first + index * wide + k
                live = jnp.where(slot < count, 1.0, 0.0).astype(F32)
                far_real = far[:side, k * side : (k + 1) * side]
                far_imag = far[side:, k * side : (k + 1) * side]
                weights.append((far_real * far_real + far_imag * far_imag - data[0, 0, slot]) * live)
            weight = jnp.concatenate(weights, 1)
            results.append(halves(jnp.concatenate([far[:side] * weight, far[side:] * weight], 0)))
        return results

    def columns_inverse(first, stacks):
        blocks = []
        for high, low in stacks:
            back_cols = tall(left_inv, high, low)
            for k in range(wide):
                block = back_cols[:, k * side : (k + 1) * side]
                blocks.append(jnp.concatenate([block[:side], block[side:]], 1))
        return halves(jnp.concatenate(blocks, 0))

    def rows_inverse(first, split):
        high, low = split
        return dot(jnp.concatenate([high, low, high], 1), right_inv[...])

    def add_back(first, chi):
        sum_real, sum_imag = grad_probe[0], grad_probe[1]
        for member in range(group):
            slot = first + member
            where, _, forth, inside = place(slot)
            chi_real = chi[member * side : (member + 1) * side, :side]
            chi_imag = chi[member * side : (member + 1) * side, side:]
            cut_real, cut_imag = patches[slot, 0], patches[slot, 1]
            sum_real = sum_real + (cut_real * chi_real + cut_imag * chi_imag)
            sum_imag = sum_imag + (cut_real * chi_imag - cut_imag * chi_real)
            grads = (
                probe_real[...] * chi_real + probe_imag[...] * chi_imag,
                probe_real[...] * chi_imag - probe_imag[...] * chi_real,
            )
            for part in range(2):
                moved = pltpu.roll(grads[part], forth, 1)
                zero = jnp.zeros_like(moved)
                grad_own[part, where, :] += pick(inside, moved, zero)
                grad_halo[part, where, :] += pick(inside, zero, moved)
        grad_probe[0], grad_probe[1] = sum_real, sum_imag

    side_by_side(
        [cut_out, rows_forward, columns_forward, columns_inverse, rows_inverse, add_back], slots, group
    )


def stage_kernel(*refs):
    count = (len(refs) - 1) // 2
    copies = [
        pltpu.make_async_copy(refs[index], refs[count + index], refs[-1].at[index])
        for index in range(count)
    ]
    for copy in copies:
        copy.start()
    for copy in copies:
        copy.wait()


def sides(partner, other, part, even):
    first, second = partner[part], other[part]
    return jnp.where(even, second, first), jnp.where(even, first, second)


def is_even():
    return lax.axis_index("tile") % 2 == 0


def load_places(sources, targets, sems):
    copies = [
        pltpu.make_async_copy(source, target, sems.at[index])
        for index, (source, target) in enumerate(zip(sources, targets))
    ]
    for copy in copies:
        copy.start()
    return copies


def fold(kept, turned, mask):
    return jnp.where(mask, kept, pltpu.roll(turned, mask.shape[-1] // 2, 1))


def pack_kernel(psi, to_partner, to_other, held, sems):
    copies = [pltpu.make_async_copy(psi.at[part, 0], held.at[part], sems.at[part]) for part in range(2)]
    for copy in copies:
        copy.start()
    mask = lane_mask(to_partner.shape, to_partner.shape[-1] // 2)
    even = is_even()
    for copy in copies:
        copy.wait()
    to_left = fold(held[0], held[1], mask)
    to_right = fold(held[0], held[1], ~mask)
    to_partner[...] = jnp.where(even, to_right, to_left)
    to_other[...] = jnp.where(even, to_left, to_right)


def unfold(low_source, high_source, mask):
    real = jnp.where(mask, low_source, high_source)
    imag = pltpu.roll(jnp.where(mask, high_source, low_source), mask.shape[-1] // 2, 1)
    return real, imag


def packed_sides(partner, other, even):
    first, second = partner[...], other[...]
    return jnp.where(even, second, first), jnp.where(even, first, second)


def first_kernel(
    pos_z, pos_x, counts, shears, psi, target, partner, other, probe, data, *rest
):
    tables = rest[:4]
    to_partner, to_other, base_out, rim_out, keep_out, send_out = rest[4:10]
    held, sems, halo, work = rest[10:12], rest[12], rest[13], rest[14:]
    copies = load_places((pos_z, pos_x), held, sems)
    pos_z, pos_x = held
    grad_own, grad_halo, grad_probe = work[:3]
    side = data.shape[-1]
    mask = lane_mask(psi.shape[2:], side // 2)
    even = is_even()
    left, right = packed_sides(partner, other, even)
    halo[0], halo[1] = unfold(right, left, mask)
    for copy in copies:
        copy.wait()
    count = counts[0, 0]
    slot_loop(
        pos_z, pos_x, count, probe.at[0], probe.at[1], data, tables, psi.at[:, 0], halo, work
    )
    for part in range(2):
        field = psi[part, 0]
        base = field - ALPHA * (grad_own[part] + RHO * (field - target[part, 0]))
        rim = -ALPHA * grad_halo[part]
        base_out[part] = base
        rim_out[part] = rim
        to_right, to_left = jnp.where(mask, rim, base), jnp.where(mask, base, rim)
        to_partner[part] = jnp.where(even, to_right, to_left)
        to_other[part] = jnp.where(even, to_left, to_right)
    row = lax.broadcasted_iota(jnp.int32, (8, side), 0)
    lane = lax.broadcasted_iota(jnp.int32, (8, side), 1)
    angle, tile = lax.axis_index("angle"), lax.axis_index("tile")
    mine = (row == 1) & (lane == angle) & (tile % inner_count(lax.axis_size("tile")) == 0)
    extra = jnp.where(row == 0, count.astype(F32), jnp.where(mine, shears[0], 0.0))
    core = angle % 2
    for out, part in ((keep_out, core), (send_out, 1 - core)):
        out[0:side] = grad_probe[part]
        out[side : side + 8] = extra


def sum_kernel(*refs):
    terms = [ref[...] for ref in refs[:-1]]
    while len(terms) > 1:
        terms = [terms[at] + terms[at + 1] for at in range(0, len(terms), 2)]
    refs[-1][...] = terms[0]


def probe_kernel(_, probe, *refs):
    total, probe_out, extra_out = refs[-1], refs[-3], refs[-2]
    sum_kernel(*refs[:-3], total)
    side = probe.shape[-1]
    extra = total[side : side + 8]
    part = lax.axis_index("angle") % 2
    probe_out[...] = probe[part] - PROBE_STEP * total[0:side] / extra[0:1]
    extra_out[...] = extra


def last_probe_kernel(probe_mine, extra, *refs):
    total, probe_out = refs[-1], refs[-2]
    sum_kernel(*refs[:-2], total)
    probe_out[...] = probe_mine[...] - PROBE_STEP * total[...] / extra[0:1]


def second_kernel(
    pos_z, pos_x, counts, base, rim, partner, other, target, probe_mine, probe_theirs, data, *rest
):
    tables = rest[:4]
    base_out, to_partner, to_other, keep_out, send_out = rest[5:10]
    inner = inner_count(lax.axis_size("tile"))
    slab_outs, rest = rest[10 : 10 + inner], rest[10 + inner :]
    held, sems, own, halo, hold, edge, probe, work = rest[:2], *rest[2:8], rest[8:]
    copies = load_places((pos_z, pos_x), held, sems)
    pos_z, pos_x = held
    grad_own, grad_halo, grad_probe = work[:3]
    side = data.shape[-1]
    mask = lane_mask(base.shape[1:], side // 2)
    tile, tiles = lax.axis_index("tile"), lax.axis_size("tile")
    from_right = jnp.where(tile < tiles - 1, 1.0, 0.0).astype(F32)
    from_left = jnp.where(tile > 0, 1.0, 0.0).astype(F32)
    core = lax.axis_index("angle") % 2
    probe[core] = probe_mine[...]
    probe[1 - core] = probe_theirs[...]
    even = is_even()
    for part in range(2):
        left, right = sides(partner, other, part, even)
        own[part] = base[part] + jnp.where(mask, left, right)
        halo[part] = jnp.where(
            mask, (right + rim[part]) * from_right, (left + rim[part]) * from_left
        )
    for copy in copies:
        copy.wait()
    slot_loop(
        pos_z, pos_x, counts[0, 0], probe.at[0], probe.at[1], data, tables, own, halo, work
    )
    for part in range(2):
        field = own[part]
        aim = target[part, 0]
        updated = field - ALPHA * (grad_own[part] + RHO * (field - aim))
        edge[part] = -ALPHA * grad_halo[part]
        base_out[part] = updated
        hold[part] = aim - updated
    to_right = fold(edge[0], edge[1], mask)
    to_left = fold(edge[0], edge[1], ~mask)
    to_partner[...] = jnp.where(even, to_right, to_left)
    to_other[...] = jnp.where(even, to_left, to_right)
    keep_out[...] = grad_probe[core]
    send_out[...] = grad_probe[1 - core]
    outer, depth = slab_outs[0].shape[0], slab_outs[0].shape[1] // 4
    for step, slab_out in enumerate(slab_outs):
        for place in range(outer):
            slab = place * inner + ((tile % inner) ^ step)
            rows = pl.ds(slab * depth, depth)
            for part in range(2):
                slab_out[place, part * depth : (part + 1) * depth] = hold[part, rows]
                slab_out[place, (2 + part) * depth : (3 + part) * depth] = edge[part, rows]


def merge_kernel(*refs):
    tile = lax.axis_index("tile")
    inner = inner_count(lax.axis_size("tile"))
    arrived, merged = refs[:inner], refs[inner:]
    for step, source in enumerate(arrived):
        for mask, out in enumerate(merged):
            out[(tile % inner) ^ step] = source[(tile // inner) ^ mask]


def forward_kernel(turn, table, _, *rest):
    *arrived, spectrum_out, rows_scratch, slabs = rest
    inner, _, width = arrived[0].shape
    tiles = slabs.shape[0]
    depth = rows_scratch.shape[0] // tiles
    outer = lax.axis_index("tile") // inner
    for mask, source in enumerate(arrived):
        slabs[pl.ds((outer ^ mask) * inner, inner)] = source[...]
    mask = lane_mask((depth, width), width // 2)
    blocks = []
    for tile in range(tiles):
        block = []
        for part in range(2):
            rows = slice((2 + part) * depth, (3 + part) * depth)
            zero = jnp.zeros((depth, width), F32)
            before = slabs[tile - 1, rows] if tile > 0 else zero
            after = slabs[tile + 1, rows] if tile < tiles - 1 else zero
            block.append(
                slabs[tile, part * depth : (part + 1) * depth] - jnp.where(mask, before, after)
            )
        blocks.append(tuple(block))
    for index, (real, imag) in enumerate(butterfly(blocks, -1)):
        cosine, sine = turn[0, index : index + 1], turn[1, index : index + 1]
        rows = slice(index * depth, (index + 1) * depth)
        rows_scratch[rows, :width] = real * cosine - imag * sine
        rows_scratch[rows, width:] = real * sine + imag * cosine
    high, low = halves(rows_scratch[...])
    spectrum = dot(jnp.concatenate([high, low, high], 1), table[...])
    count = rows_scratch.shape[0]
    spectrum_out[0:count] = spectrum[:, :width]
    spectrum_out[count : 2 * count] = spectrum[:, width:]


def phase_kernel(tiles, sums, table_out):
    angles, _, _, beam, width = table_out.shape
    total = tiles * width
    first = lax.axis_index("angle") * beam - (beam * lax.axis_size("angle")) // 2
    offsets = (lax.broadcasted_iota(jnp.int32, (beam, width), 0) + first).astype(F32)
    column = lax.broadcasted_iota(jnp.int32, (beam, width), 1)
    for angle in range(angles):
        shear = sums[sums.shape[0] - 7 : sums.shape[0] - 6, angle : angle + 1]
        for block in range(tiles):
            frequency = block + tiles * column
            signed = jnp.where(frequency < total // 2, frequency, frequency - total).astype(F32)
            turns = (offsets * signed * shear) * (1.0 / total)
            turns = turns - jnp.floor(turns + 0.5)
            x = turns * math.pi
            square = x * x
            sine = x * (
                1.0 + square * (-1 / 6 + square * (1 / 120 + square * (-1 / 5040 + square * (
                    1 / 362880 + square * (-1 / 39916800 + square * (1.0 / 6227020800.0))))))
            )
            cosine = 1.0 + square * (-1 / 2 + square * (1 / 24 + square * (-1 / 720 + square * (
                1 / 40320 + square * (-1 / 3628800 + square * (1.0 / 479001600.0))))))
            real = 1.0 - 2.0 * sine * sine
            imag = 2.0 * sine * cosine
            table_out[angle, 0, block] = real
            table_out[angle, 1, block] = imag - real
            table_out[angle, 2, block] = real + imag


def inverse_kernel(depth, masks, phases, turn, table, *rest):
    spectra = rest[: len(masks)]
    image_out, token, image, sems = rest[-4:]
    token[...] = jnp.zeros_like(token)
    _, _, tiles, beam, width = phases.shape
    angles = [lax.axis_index("angle") ^ mask for mask in masks]
    copies = []
    wide = math.gcd(depth, 2)
    count = tiles * depth

    def sum_angles(start, _):
        rows = [[] for _ in range(wide)]
        for block in range(tiles):
            tables = [[phases[angle, which, block] for which in range(3)] for angle in angles]
            for member in range(wide):
                at = block * depth + start + member
                sums = None
                for spectrum, three in zip(spectra, tables):
                    real = spectrum[pl.ds(at, 1), :]
                    imag = spectrum[pl.ds(count + at, 1), :]
                    terms = [factor * one for factor, one in zip((real + imag, real, imag), three)]
                    sums = terms if sums is None else [x + y for x, y in zip(sums, terms)]
                rows[member].append(jnp.concatenate([sums[0] - sums[2], sums[0] + sums[1]], 1))
        return [halves(jnp.concatenate(blocks, 0)) for blocks in rows]

    def transform(start, splits):
        return [dot(jnp.concatenate([high, low, high], 1), table[...]) for high, low in splits]

    def store(start, images):
        for member, one in enumerate(images):
            blocks = []
            for block in range(tiles):
                real = one[block * beam : (block + 1) * beam, :width]
                imag = one[block * beam : (block + 1) * beam, width:]
                cosine, sine = turn[0, block : block + 1], turn[1, block : block + 1]
                blocks.append((real * cosine - imag * sine, real * sine + imag * cosine))
            for index, (real, imag) in enumerate(butterfly(blocks, 1)):
                columns = slice(index * width, (index + 1) * width)
                image[0, start + member, :, columns] = real.astype(BF16)
                image[1, start + member, :, columns] = imag.astype(BF16)
        rows = pl.ds(start, wide)
        copy = pltpu.make_async_copy(image.at[:, rows], image_out.at[:, rows], sems.at[start // wide])
        copy.start()
        copies.append(copy)

    side_by_side([sum_angles, transform, store], depth, wide)
    for copy in copies:
        copy.wait()


def finish_kernel(base, partner, other, probe_mine, probe_theirs, _, psi_out, probe_out):
    mask = lane_mask(base.shape[1:], base.shape[-1] // 2)
    left, right = packed_sides(partner, other, is_even())
    real, imag = unfold(left, right, mask)
    psi_out[0, 0] = base[0] + real
    psi_out[1, 0] = base[1] + imag
    core = lax.axis_index("angle") % 2
    probe_out[core] = probe_mine[...]
    probe_out[1 - core] = probe_theirs[...]


VMEM = pl.BlockSpec(memory_space=pltpu.VMEM)
SMEM = pl.BlockSpec(memory_space=pltpu.SMEM)
HBM = pl.BlockSpec(memory_space=pltpu.HBM)
ANY = pl.BlockSpec(memory_space=pl.ANY)


def call(body, name, out_shape, in_specs, scratch=(), flops=0, size=0, **more):
    return pl.pallas_call(
        body,
        name=name,
        out_shape=out_shape,
        in_specs=in_specs,
        scratch_shapes=list(scratch),
        compiler_params=pltpu.CompilerParams(vmem_limit_bytes=VMEM_LIMIT),
        cost_estimate=pl.CostEstimate(flops=flops, bytes_accessed=size, transcendentals=0),
        **more,
    )


def shape(*dims, dtype=F32):
    return jax.ShapeDtypeStruct(dims, dtype)


def swap_pairs(array, start, tiles):
    low = range(start, tiles - 1, 2)
    return lax.ppermute(array, "tile", [(i, i + 1) for i in low] + [(i + 1, i) for i in low])


def exchange(to_partner, to_other, tiles):
    return swap_pairs(to_partner, 0, tiles), swap_pairs(to_other, 1, tiles)


def inner_count(tiles):
    return max(1, tiles // 4)


def swap(array, mask, devices):
    return lax.ppermute(array, ("angle", "tile"), [(i, i ^ mask) for i in range(devices)])


def hypercube(angles, tiles):
    bits = [tiles << at for at in range(1, angles.bit_length() - 1)]
    bits += [1 << at for at in range(tiles.bit_length() - 1)]
    rounds = []
    while bits:
        two, bits = bits[:2], bits[2:]
        rounds.append(two if len(two) == 1 else [two[0], two[1], two[0] ^ two[1]])
    return rounds


def shards(psi, target, probe, data, pos_z, pos_x, counts, shears):
    rows_total, width = psi.shape[2], psi.shape[3]
    side = probe.shape[1]
    angles, tiles = lax.axis_size("angle"), lax.axis_size("tile")
    devices = angles * tiles
    depth = rows_total // tiles
    beam = 32
    norm = 1.0 / math.sqrt(side)
    tables = [
        jnp.asarray(right_table(side, -1.0, norm)),
        jnp.asarray(left_table(side, -1.0, norm)),
        jnp.asarray(left_table(side, 1.0, norm)),
        jnp.asarray(right_table(side, 1.0, norm)),
    ]
    block = (2, rows_total, width)
    work = [
        pltpu.VMEM(block, F32),
        pltpu.VMEM(block, F32),
        pltpu.VMEM((2, side, side), F32),
        pltpu.VMEM((data.shape[2], 2, side, side), F32),
    ]
    slots = data.shape[2]
    flops = slots * 4 * 2 * side * 6 * side * 2 * side
    slot_places = [pltpu.with_memory_space_constraint(x, pltpu.HBM) for x in (pos_z, pos_x)]
    places = [pltpu.SMEM(x.shape, x.dtype) for x in slot_places] + [pltpu.SemaphoreType.DMA((2,))]
    psi = pltpu.with_memory_space_constraint(psi, pltpu.HBM)
    flat = shape(rows_total, width)
    to_partner, to_other = call(
        pack_kernel,
        "psi_pack",
        [flat] * 2,
        [HBM],
        [pltpu.VMEM(block, F32), pltpu.SemaphoreType.DMA((2,))],
    )(psi)
    partner, other = exchange(to_partner, to_other, tiles)
    operands = [
        pltpu.with_memory_space_constraint(x, pltpu.HBM)
        for x in [psi, target, probe, data] + tables
    ]
    psi_in, target_in, probe_in, data_in, *tables = call(
        stage_kernel,
        "stage_operands",
        [pltpu.VMEM(x.shape, x.dtype) for x in operands],
        [HBM] * len(operands),
        [pltpu.SemaphoreType.DMA((len(operands),))],
        0,
        3_000_000,
        out_specs=[VMEM] * len(operands),
    )(*operands)
    target_in, data_in, *tables = [
        pltpu.with_memory_space_constraint(x, pltpu.VMEM) for x in [target_in, data_in] + tables
    ]
    half = shape(side + 8, side)
    to_partner, to_other, base, rim, keep, send = call(
        first_kernel,
        "ptycho_first",
        [shape(*block)] * 4 + [half] * 2,
        [HBM] * 2 + [SMEM] * 2 + [VMEM] * 10,
        places + [pltpu.VMEM(block, F32)] + work,
        flops,
    )(*slot_places, counts, shears, psi_in, target_in, partner, other, probe_in, data_in, *tables)
    rounds = hypercube(angles, tiles)

    def all_but_last(keep, send, rounds):
        piece = shape(*keep.shape)
        total = call(sum_kernel, "probe_sum", piece, [VMEM] * 2)(keep, swap(send, tiles, devices))
        for masks in rounds[:-1]:
            terms = [total] + [swap(total, mask, devices) for mask in masks]
            total = call(sum_kernel, "probe_sum", piece, [VMEM] * len(terms))(*terms)
        return total

    def last_round(total, rounds):
        return [total] + [swap(total, mask, devices) for mask in rounds[-1]]

    nearly = all_but_last(keep, send, rounds)
    terms = last_round(nearly, rounds)
    partner, other = exchange(to_partner, to_other, tiles)
    phases = call(
        functools.partial(phase_kernel, tiles),
        "phase_table",
        shape(angles, 3, tiles, beam, width),
        [VMEM],
        (),
        angles * tiles * beam * width * 40,
    )(nearly)
    probe_mine, extra = call(
        probe_kernel,
        "probe_step",
        [shape(side, side), shape(8, side)],
        [ANY] + [VMEM] * (1 + len(terms)),
        [pltpu.VMEM((side + 8, side), F32)],
    )(phases, probe_in, *terms)
    probe_theirs = swap(probe_mine, tiles, devices)
    inner = inner_count(tiles)
    outer = tiles // inner
    base, to_partner, to_other, keep, send, *slabs = call(
        second_kernel,
        "ptycho_second",
        [shape(*block), flat, flat]
        + [shape(side, side)] * 2
        + [shape(outer, 4 * depth, width)] * inner,
        [HBM] * 2 + [SMEM] + [VMEM] * 12 + [ANY],
        places + [pltpu.VMEM(block, F32)] * 4 + [pltpu.VMEM((2, side, side), F32)] + work,
        flops,
    )(
        *(*slot_places, counts, base, rim, partner, other, target_in),
        *(probe_mine, probe_theirs, data_in, *tables, phases),
    )
    slabs = slabs[:1] + [swap(array, mask + 1, devices) for mask, array in enumerate(slabs[1:])]
    slabs = call(
        merge_kernel, "slab_merge", [shape(inner, 4 * depth, width)] * outer, [VMEM] * inner
    )(*slabs)
    slabs = [slabs[0]] + [swap(array, (mask + 1) * inner, devices) for mask, array in enumerate(slabs[1:])]
    total = all_but_last(keep, send, rounds)
    late, to_other = lax.optimization_barrier((total, to_other))
    other = swap_pairs(to_other, 1, tiles)
    for mask in rounds[-1][: 1 if len(rounds[-1]) > 1 else 0]:
        late = call(sum_kernel, "probe_sum", shape(*late.shape), [VMEM] * 2)(
            late, swap(late, mask, devices)
        )
    count = tiles * depth
    spectrum = call(
        forward_kernel,
        "slab_spectrum",
        shape(2 * count, width),
        [VMEM] * 2 + [ANY] + [VMEM] * outer,
        [pltpu.VMEM((count, 2 * width), F32), pltpu.VMEM((tiles, 4 * depth, width), F32)],
    )(
        jnp.asarray(twiddles(tiles, width, -1.0, 1.0)),
        jnp.asarray(right_table(width, -1.0, 1.0)),
        late,
        *slabs,
    )
    masks = list(range(angles))
    spectra = [spectrum] + [swap(spectrum, mask * tiles, devices) for mask in masks[1:]]
    late, spectra[1], to_partner = lax.optimization_barrier((late, spectra[1], to_partner))
    terms = [late, swap(late, rounds[-1][min(1, len(rounds[-1]) - 1)], devices)]
    partner = swap_pairs(to_partner, 0, tiles)
    probe_mine = call(
        last_probe_kernel,
        "probe_last",
        shape(side, side),
        [VMEM] * (2 + len(terms)),
        [pltpu.VMEM((side, side), F32)],
    )(probe_mine, extra, *terms)
    probe_theirs = swap(probe_mine, tiles, devices)
    scale = 1.0 / (angles * tiles * width)
    tomo, token = call(
        functools.partial(inverse_kernel, depth, masks),
        "slab_image",
        [shape(2, depth, beam, tiles * width, dtype=BF16), shape(8, width)],
        [VMEM] * (3 + angles) + [ANY],
        [
            pltpu.VMEM((2, depth, beam, tiles * width), BF16),
            pltpu.SemaphoreType.DMA((depth // math.gcd(depth, 2),)),
        ],
        depth * tiles * beam * 2 * 6 * width * 2 * width,
        out_specs=[HBM, VMEM],
    )(
        phases,
        jnp.asarray(twiddles(tiles, width, 1.0, scale)),
        jnp.asarray(right_table(width, 1.0, 1.0)),
        *spectra,
        probe_mine,
    )
    psi_new, probe_new = call(
        finish_kernel,
        "field_probe",
        [shape(2, 1, rows_total, width), shape(2, side, side)],
        [VMEM] * 5 + [ANY],
    )(base, partner, other, probe_mine, probe_theirs, token)
    return psi_new, probe_new, tomo


def solution(mesh):
    in_specs = (
        P(None, "angle", None, "tile"),
        P(None, "angle", None, "tile"),
        P(),
        P("angle", "tile", None, None, None),
        P("angle", "tile", None),
        P("angle", "tile", None),
        P("angle", "tile"),
        P("angle"),
    )
    out_specs = (P(None, "angle", None, "tile"), P(), P(None, "tile", "angle", None))
    return jax.shard_map(shards, mesh=mesh, in_specs=in_specs, out_specs=out_specs, check_vma=False)
```
